512 devices in a mesh: cp: 64 (over z_hi, y, core), tp: 8 (over x, z_lo).
Axes of the slice: x: 4, y: 8, z: 8 (z_hi: 4, z_lo: 2; z = z_hi * 2 + z_lo), core: 2. Of those that a mesh axis runs over, the one named last changes fastest.
Arguments:
- query_rows: bfloat16 [128, 256, 8192], P('cp', 'tp'), may hold values from -6 to 6
- key_rows: bfloat16 [128, 256, 1024], P('cp', 'tp'), may hold values from -6 to 6
- value_matrix: bfloat16 [128, 256, 1024], P('cp', 'tp'), may hold values from -6 to 6
- doc_start: int32 [128, 256], P('cp'), may hold values from 0 to 32767, as said below
- source_lists: int32 [128, 2], P('cp'), may hold values from -1 to 126, as said below
- slot_block: int32 [128], replicated, may hold values from 0 to 127, as said below
Outputs:
- attended: bfloat16 [128, 256, 8192], P('cp', None, 'tp')
The draws below stay inside these ranges and needn't reach their ends.
Inputs may be any that keep to these rules, and one draw needn't show every extreme that they name: Documents lie end to end over the 32768 positions, each of 1 to 512 tokens and at least one of exactly 512; doc_start is constant within a document and equals the position of its first token. `source_lists`: the list of block b is b - 1, b - 2, ... down to the block that holds the document start of b's first token, then -1 to the end; some block names exactly 2 blocks. `slot_block`: cp device c holds blocks c and 127 - c in its 2 slots, in an order that is drawn for each device.
All inputs are finite; a program needn't handle non-finite values.
Results may differ from the reference program's by a relative error of at most 0.0035.
Values may be sent and summed in bfloat16 or wider, within the bound.
A program may use at most 64 MiB of HBM per device.

```python
import jax
import jax.numpy as jnp
from jax import lax

QUERY_HEAD_COUNT = 64
KEY_VALUE_HEADS = 8
HEAD_SIZE = 128
BLOCK_TOKENS = 256
NB = 2
LIST = 2
BLOCK_COUNT = 128


def layout(key):
    total = BLOCK_COUNT * BLOCK_TOKENS
    longest = LIST * BLOCK_TOKENS
    first = jax.random.randint(jax.random.fold_in(key, 101), (), 1, BLOCK_TOKENS)
    last = 1
    lengths = jax.random.randint(jax.random.fold_in(key, 103), (total,), 1, longest + 1)
    ends = jnp.cumsum(lengths)
    begin = first + longest
    middle = total - last - longest - begin
    places = jnp.where(ends - lengths < middle, begin + ends - lengths, total)
    fixed_starts = jnp.stack([jnp.zeros((), jnp.int32), first, begin, begin + middle, jnp.asarray(total - last, jnp.int32)]).astype(jnp.int32)
    marks = jnp.zeros((total,), jnp.int32).at[places].max(1, mode='drop')
    marks = marks.at[fixed_starts].max(1)
    positions = jnp.arange(total, dtype=jnp.int32)
    doc_first = lax.cummax(jnp.where(marks > 0, positions, 0), axis=0)
    block_ids = jnp.arange(BLOCK_COUNT, dtype=jnp.int32)
    reach_back = block_ids - doc_first[block_ids * BLOCK_TOKENS] // BLOCK_TOKENS
    steps_back = jnp.arange(LIST, dtype=jnp.int32)
    lists = jnp.where(steps_back[None, :] < reach_back[:, None], block_ids[:, None] - 1 - steps_back[None, :], -1)
    devices = BLOCK_COUNT // NB
    flips = jax.random.randint(jax.random.fold_in(key, 104), (devices,), 0, 2)
    lower_half = jnp.arange(devices, dtype=jnp.int32)
    upper_half = BLOCK_COUNT - 1 - lower_half
    first_slot = jnp.where(flips > 0, upper_half, lower_half)
    second_slot = jnp.where(flips > 0, lower_half, upper_half)
    order = jnp.stack([first_slot, second_slot], axis=1).reshape(BLOCK_COUNT)
    return (doc_first.reshape(BLOCK_COUNT, BLOCK_TOKENS)[order], lists[order].astype(jnp.int32), order)


def draw_query_rows(key, part):
    key = jax.random.fold_in(key, 5)
    base_offset = jnp.clip(jax.random.normal(key, (BLOCK_COUNT, BLOCK_TOKENS, QUERY_HEAD_COUNT * HEAD_SIZE), jnp.float32), -6.0, 6.0)
    return base_offset.astype(jnp.bfloat16)


def draw_key_rows(key, part):
    key = jax.random.fold_in(key, 6)
    base_offset = jnp.clip(jax.random.normal(key, (BLOCK_COUNT, BLOCK_TOKENS, KEY_VALUE_HEADS * HEAD_SIZE), jnp.float32), -6.0, 6.0)
    return base_offset.astype(jnp.bfloat16)


def draw_doc_start(key, part):
    starts, lists, order = layout(key)
    return starts.astype(jnp.int32)


def draw_source_lists(key, part):
    starts, lists, order = layout(key)
    return lists.astype(jnp.int32)


def draw_slot_block(key, part):
    starts, lists, order = layout(key)
    return order.astype(jnp.int32)


def block_scale(rng, extent, shards, smallest, high):
    loudness, own = 1.0, jax.random.fold_in(rng, 6)
    for position, blocks in shards:
        draws = jnp.exp(jax.random.uniform(jax.random.fold_in(own, position), (blocks,), jnp.float32, smallest / len(shards), high / len(shards)))
        loudness = loudness * jnp.repeat(draws, extent[position] // blocks).reshape([-1 if axis == position else 1 for axis in range(len(extent))])
    return loudness


def noise(rng, dims, scale, reach, cuts=(), kind=jnp.bfloat16):
    drawn = jax.random.normal(rng, dims, jnp.float32) * scale
    if len(cuts) > 0:
        drawn = block_scale(rng, dims, cuts, -0.22, 0.18) * drawn
    return jnp.clip(drawn, min=-reach, max=reach).astype(kind)


def setup_inputs(seed: int = 0) -> dict:
    key_of = jax.random.split(jax.random.key(seed), 7)
    query_rows = draw_query_rows(jax.random.fold_in(key_of[6], 71), 0)
    key_rows = draw_key_rows(jax.random.fold_in(key_of[6], 71), 0)
    value_matrix = noise(key_of[2], (BLOCK_COUNT, BLOCK_TOKENS, KEY_VALUE_HEADS * HEAD_SIZE), 1.0, 6.0, ((0, 64), (1, 8)))
    doc_start = draw_doc_start(jax.random.fold_in(key_of[6], 71), 0)
    source_lists = draw_source_lists(jax.random.fold_in(key_of[6], 71), 0)
    slot_block = draw_slot_block(jax.random.fold_in(key_of[6], 71), 0)
    return {"query_rows": query_rows, "key_rows": key_rows, "value_matrix": value_matrix, "doc_start": doc_start, "source_lists": source_lists, "slot_block": slot_block}


neg_large = -1.0e30


def attend_block(query_tile_rows, key_collection, value_collection, visible):
    token_list = query_tile_rows.shape[0]
    query_group = QUERY_HEAD_COUNT // KEY_VALUE_HEADS
    query_fourth = query_tile_rows.reshape(token_list, KEY_VALUE_HEADS, query_group, HEAD_SIZE).astype(jnp.float32)
    key_third = key_collection.reshape(-1, KEY_VALUE_HEADS, HEAD_SIZE).astype(jnp.float32)
    value_third = value_collection.reshape(-1, KEY_VALUE_HEADS, HEAD_SIZE).astype(jnp.float32)
    scores = jnp.einsum("qagd,kad->agqk", query_fourth, key_third) * (HEAD_SIZE ** -0.5)
    scores = jnp.where(visible[None, None], scores, neg_large)
    weights = jnp.exp(scores - jnp.max(scores, axis=-1, keepdims=True))
    total = jnp.sum(weights, axis=-1)
    probs = lax.optimization_barrier(weights.astype(jnp.bfloat16)).astype(jnp.float32)
    mixed = jnp.einsum("agqk,kad->agqd", probs, value_third) / total[..., None]
    return jnp.transpose(mixed, (2, 0, 1, 3)).reshape(token_list, QUERY_HEAD_COUNT * HEAD_SIZE).astype(jnp.bfloat16)


def reference(query_rows, key_rows, value_matrix, doc_start, source_lists, slot_block):
    slots = slot_block.shape[0]
    inverse = jnp.zeros((slots,), jnp.int32).at[slot_block].set(jnp.arange(slots, dtype=jnp.int32))
    offsets = jnp.arange(BLOCK_TOKENS, dtype=jnp.int32)

    def one_slot(items):
        query_tile_rows, starts, listed, block_id = items
        chosen = jnp.concatenate([block_id[None], listed]).astype(jnp.int32)
        valid = jnp.concatenate([jnp.ones((1,), jnp.bool_), listed >= 0])
        holders = inverse[jnp.maximum(chosen, 0)]
        key_collection = key_rows[holders].reshape(-1, key_rows.shape[2])
        value_collection = value_matrix[holders].reshape(-1, value_matrix.shape[2])
        key_pos = (chosen[:, None] * BLOCK_TOKENS + offsets[None, :]).reshape(-1)
        valid_pos = jnp.repeat(valid, BLOCK_TOKENS)
        query_pos = block_id * BLOCK_TOKENS + offsets
        visible = valid_pos[None, :] & (key_pos[None, :] <= query_pos[:, None]) & (key_pos[None, :] >= starts[:, None])
        return attend_block(query_tile_rows, key_collection, value_collection, visible)

    return lax.map(one_slot, (query_rows, doc_start, source_lists, slot_block))
```

```python
import functools

import jax
import jax.numpy as jnp
from jax import lax
from jax.experimental import pallas as pl
from jax.experimental.pallas import tpu as pltpu
from jax.sharding import PartitionSpec as P

QUERY_HEAD_COUNT = 64
KEY_VALUE_HEADS = 8
HEAD_SIZE = 128
LIST = 2
MESH = pl.DeviceIdType.MESH

neg_large = -1e30
SCALE = HEAD_SIZE ** (-0.5) * 1.4426950408889634
RUN = 2
ORDER = (0, 1, 2, 3, 6, 7, 4, 5)


def kernel(
    n_cp,
    n_tp,
    q_hbm,
    k_hbm,
    v_hbm,
    start_hbm,
    list_hbm,
    slot_hbm,
    out_hbm,
    q_all,
    k_all,
    v_all,
    stage,
    inbox,
    out_buf,
    start_buf,
    low_bound,
    list_buf,
    slot_buf,
    small_sem,
    own_sem,
    kv_send,
    kv_recv,
    q_send,
    q_recv,
    far_send,
    far_recv,
    out_sem,
):
    held, part, _ = q_hbm.shape
    tokens = part * n_tp
    width = q_hbm.shape[2] // n_tp
    kv_width = k_hbm.shape[2] // n_tp
    group = width // HEAD_SIZE
    window = LIST * tokens + tokens // 2
    c = lax.axis_index("cp")
    t = lax.axis_index("tp")
    n_x = n_tp // RUN
    x, z = t // RUN, t % RUN

    def peer(offset, sign):
        dx, dz = offset // RUN, offset % RUN
        return ((x + sign * dx + n_x) % n_x) * RUN + (z + sign * dz + RUN) % RUN

    barrier = pltpu.get_barrier_semaphore()
    for offset in range(1, n_tp):
        pl.semaphore_signal(
            barrier, inc=1, device_id=(c, peer(offset, 1)), device_id_type=MESH
        )
    for step in (1, 2):
        for side in (-1, 1):
            other = c + side * step

            @pl.when((other >= 0) & (other < n_cp))
            def _():
                pl.semaphore_signal(barrier, inc=1, device_id=(other, t), device_id_type=MESH)

    small = [
        pltpu.make_async_copy(start_hbm, start_buf, small_sem.at[0]),
        pltpu.make_async_copy(list_hbm, list_buf, small_sem.at[1]),
        pltpu.make_async_copy(slot_hbm, slot_buf, small_sem.at[2]),
    ]
    own_rows = pl.ds(pl.multiple_of(t * part, part), part)
    own_key_rows = pl.ds(pl.multiple_of(LIST * tokens + t * part, part), part)

    def cut(ref, size, which):
        return ref.at[:, :, pl.ds(pl.multiple_of(which * size, size), size)]

    own = [
        pltpu.make_async_copy(cut(q_hbm, width, t), q_all.at[:, own_rows], own_sem.at[0]),
        pltpu.make_async_copy(cut(k_hbm, kv_width, t), k_all.at[:, own_key_rows], own_sem.at[1]),
        pltpu.make_async_copy(cut(v_hbm, kv_width, t), v_all.at[:, own_key_rows], own_sem.at[2]),
    ]
    for copy in small + own:
        copy.start()

    greeted = n_tp - 1
    for step in (1, 2):
        greeted = greeted + jnp.where(c >= step, 1, 0) + jnp.where(c + step < n_cp, 1, 0)
    pl.semaphore_wait(barrier, greeted)

    kv_copies = []
    q_copies = {}
    for offset in range(1, n_tp):
        to = peer(offset, 1)
        for which, (ref, dst) in enumerate(((k_hbm, k_all), (v_hbm, v_all))):
            kv_copies.append(
                pltpu.make_async_remote_copy(
                    src_ref=cut(ref, kv_width, to),
                    dst_ref=dst.at[:, own_key_rows],
                    send_sem=kv_send.at[which, offset],
                    recv_sem=kv_recv.at[which, offset],
                    device_id=(c, to),
                    device_id_type=MESH,
                )
            )
            kv_copies[-1].start()
    for offset in ORDER[1:]:
        to = peer(offset, 1)
        q_copies[offset] = pltpu.make_async_remote_copy(
            src_ref=cut(q_hbm, width, to),
            dst_ref=q_all.at[:, own_rows],
            send_sem=q_send.at[offset],
            recv_sem=q_recv.at[offset],
            device_id=(c, to),
            device_id_type=MESH,
        )
        q_copies[offset].start()

    for copy in small:
        copy.wait()
    upper = []
    for s in range(held):
        block_id = slot_buf[c * held + s]
        upper.append(jnp.where(block_id >= n_cp, 1, 0))
        named = jnp.int32(0)
        for entry in range(LIST):
            named = named + jnp.where(list_buf[s, entry] >= 0, tokens, 0)
        row = jnp.maximum(start_buf[s : s + 1, :] - block_id * tokens, -named)
        for at in range(0, tokens, 128):
            low_bound[s, at : at + 128, :] = jnp.broadcast_to(
                row[:, at : at + 128], (128, 128)
            ).T

    own[1].wait()
    own[2].wait()
    for copy in kv_copies:
        copy.wait_recv()
    for place in range(held):
        slot = (upper[0] + place) % held
        stage[place, 0] = k_all[slot, pl.ds(LIST * tokens, tokens), :]
        stage[place, 1] = v_all[slot, pl.ds(LIST * tokens, tokens), :]

    def far(place, box, side, step):
        return pltpu.make_async_remote_copy(
            src_ref=stage.at[place],
            dst_ref=inbox.at[box],
            send_sem=far_send.at[box],
            recv_sem=far_recv.at[box],
            device_id=(c + side * step, t),
            device_id_type=MESH,
        )

    for step in (1, 2):

        @pl.when(c + step < n_cp)
        def _():
            far(0, step - 1, 1, step).start()

        @pl.when(c >= step)
        def _():
            far(1, step + 1, -1, step).start()

        @pl.when(c < step)
        def _():
            inbox[step - 1] = jnp.zeros(inbox.shape[1:], inbox.dtype)

    @pl.when(c == n_cp - 1)
    def _():
        far(0, 3, -1, 1).start()
        inbox[2] = stage[0]

    for step in (1, 2):

        @pl.when(c >= step)
        def _():
            far(0, step - 1, 1, step).wait_recv()

    @pl.when(c < n_cp - 1)
    def _():
        far(1, 2, -1, 1).wait_recv()
        far(1, 3, -1, 2).wait_recv()

    @pl.when(c == n_cp - 1)
    def _():
        inbox[3] = inbox[0]

    for s in range(held):
        for step in (1, 2):
            box = upper[s] * 2 + step - 1
            rows = pl.ds((LIST - step) * tokens, tokens)
            k_all[s, rows, :] = inbox[box, 0]
            v_all[s, rows, :] = inbox[box, 1]

    lane = lax.broadcasted_iota(jnp.int32, (part, 128), 1)
    sub = lax.broadcasted_iota(jnp.int32, (part, 128), 0)

    def attend(s, source):
        rows = pl.ds(pl.multiple_of(source * part, part), part)
        first = (source // (n_tp // 2)) * (tokens // 2)
        keys = pl.ds(pl.multiple_of(first, tokens // 2), window)
        query = q_all[s, rows, :]
        query = jnp.concatenate(
            [query[:, h * HEAD_SIZE : (h + 1) * HEAD_SIZE] for h in range(group)], axis=0
        )
        scores = lax.dot_general(
            query, k_all[s, keys, :], (((1,), (1,)), ((), ())), preferred_element_type=jnp.float32
        )
        lowest = low_bound[s, rows, :]
        highest = sub + source * part
        visible = []
        for at in range(0, window, 128):
            key = lane + (first + at - LIST * tokens)
            visible.append((key >= lowest) & (key <= highest))
        visible = jnp.concatenate(visible, axis=1)
        scores = scores.reshape(group, part, window)
        scores = jnp.where(visible[None], scores, neg_large)
        scores = scores.reshape(group * part, window)
        best = jnp.max(scores, axis=-1, keepdims=True)
        weights = jnp.exp2((scores - best) * SCALE)
        total = jnp.sum(weights, axis=-1, keepdims=True)
        mixed = jnp.dot(
            weights.astype(jnp.bfloat16), v_all[s, keys, :], preferred_element_type=jnp.float32
        )
        mixed = (mixed * (1.0 / total)).astype(jnp.bfloat16)
        for h in range(group):
            out_buf[s, rows, h * HEAD_SIZE : (h + 1) * HEAD_SIZE] = mixed[
                h * part : (h + 1) * part
            ]

    out_copies = []
    for offset in ORDER:
        if offset == 0:
            own[0].wait()
        else:
            q_copies[offset].wait_recv()
        source = peer(offset, -1)
        for s in range(held):
            attend(s, source)
        rows = pl.ds(pl.multiple_of(source * part, part), part)
        copy = pltpu.make_async_copy(
            out_buf.at[:, rows], out_hbm.at[:, rows], out_sem.at[offset]
        )
        copy.start()
        out_copies.append(copy)

    for copy in kv_copies:
        copy.wait_send()
    for copy in q_copies.values():
        copy.wait_send()
    for step in (1, 2):

        @pl.when(c + step < n_cp)
        def _():
            far(0, step - 1, 1, step).wait_send()

        @pl.when(c >= step)
        def _():
            far(1, step + 1, -1, step).wait_send()

    @pl.when(c == n_cp - 1)
    def _():
        far(0, 3, -1, 1).wait_send()

    for copy in out_copies:
        copy.wait()


def on_device(n_cp, n_tp, query_rows, key_rows, value_matrix, doc_start, source_lists, slot_block):
    held, part, all_width = query_rows.shape
    tokens = part * n_tp
    width = all_width // n_tp
    kv_width = key_rows.shape[2] // n_tp
    reach = (LIST + 1) * tokens
    bf16, i32 = jnp.bfloat16, jnp.int32
    dma = pltpu.SemaphoreType.DMA
    return pl.pallas_call(
        functools.partial(kernel, n_cp, n_tp),
        out_shape=jax.ShapeDtypeStruct((held, tokens, width), bf16),
        in_specs=[pl.BlockSpec(memory_space=pltpu.HBM)] * 6,
        out_specs=pl.BlockSpec(memory_space=pl.ANY),
        scratch_shapes=[
            pltpu.VMEM((held, tokens, width), bf16),
            pltpu.VMEM((held, reach, kv_width), bf16),
            pltpu.VMEM((held, reach, kv_width), bf16),
            pltpu.VMEM((2, 2, tokens, kv_width), bf16),
            pltpu.VMEM((4, 2, tokens, kv_width), bf16),
            pltpu.VMEM((held, tokens, width), bf16),
            pltpu.VMEM((held, tokens), i32),
            pltpu.VMEM((held, tokens, 128), i32),
            pltpu.SMEM(source_lists.shape, i32),
            pltpu.SMEM(slot_block.shape, i32),
            dma((3,)),
            dma((3,)),
            dma((2, n_tp)),
            dma((2, n_tp)),
            dma((n_tp,)),
            dma((n_tp,)),
            dma((4,)),
            dma((4,)),
            dma((n_tp,)),
        ],
        compiler_params=pltpu.CompilerParams(
            collective_id=0, has_side_effects=True, vmem_limit_bytes=40 * 1024 * 1024
        ),
        name="attention",
    )(query_rows, key_rows, value_matrix, doc_start, source_lists, slot_block)


def solution(mesh):
    in_specs = (
        P("cp", "tp", None),
        P("cp", "tp", None),
        P("cp", "tp", None),
        P("cp", None),
        P("cp", None),
        P(),
    )
    out_specs = P("cp", None, "tp")
    return jax.shard_map(
        functools.partial(on_device, mesh.shape["cp"], mesh.shape["tp"]),
        mesh=mesh,
        in_specs=in_specs,
        out_specs=out_specs,
        check_vma=False,
    )
```

```python
import functools

import jax
import jax.numpy as jnp
from jax import lax
from jax.experimental import pallas as pl
from jax.experimental.pallas import tpu as pltpu
from jax.sharding import PartitionSpec as P

QUERY_HEAD_COUNT = 64
KEY_VALUE_HEADS = 8
HEAD_SIZE = 128
LIST = 2
MESH = pl.DeviceIdType.MESH

neg_large = -1e30
SCALE = HEAD_SIZE ** (-0.5) * 1.4426950408889634
RUN = 2
ORDER = (1, 2, 6, 3, 7, 4, 5)
AHEAD = 3
GROUP = 16
LEGS = (GROUP, 2 - GROUP)


def kernel(
    n_cp,
    n_tp,
    q_hbm,
    k_hbm,
    v_hbm,
    start_hbm,
    list_hbm,
    slot_hbm,
    out_ref,
    q_all,
    k_all,
    v_all,
    stage,
    inbox,
    relay,
    start_buf,
    low_bound,
    list_buf,
    slot_buf,
    small_sem,
    own_sem,
    kv_send,
    kv_recv,
    q_send,
    q_recv,
    far_send,
    far_recv,
    relay_recv,
):
    held, part, _ = q_hbm.shape
    tokens = part * n_tp
    width = q_hbm.shape[2] // n_tp
    kv_width = k_hbm.shape[2] // n_tp
    group = width // HEAD_SIZE
    window = LIST * tokens + tokens // 2
    c = lax.axis_index("cp")
    t = lax.axis_index("tp")
    n_x = n_tp // RUN
    x, z = t // RUN, t % RUN

    def peer(offset, sign):
        dx, dz = offset // RUN, offset % RUN
        return ((x + sign * dx + n_x) % n_x) * RUN + (z + sign * dz + RUN) % RUN

    def climbs(who):
        return (who >= 0) & (who + GROUP < n_cp) & ((who + 2 * GROUP) % GROUP == GROUP - 2)

    def descends(who):
        return (who >= GROUP) & (who < n_cp) & (who % GROUP == 1)

    leg, rest = LEGS
    even = c % 2 == 0
    odd = c % 2 == 1
    relays_low, relays_high = climbs(c - leg), descends(c + leg)

    partners = [
        (c >= 1, -1),
        (c >= 2, -2),
        (c + 1 < n_cp, 1),
        (c + 2 < n_cp, 2),
        (climbs(c), leg),
        (relays_low, -leg),
        (relays_low, rest),
        (climbs(c - leg - rest), -rest),
        (descends(c), -leg),
        (relays_high, leg),
        (relays_high, -rest),
        (descends(c + leg + rest), rest),
    ]
    barrier = pltpu.get_barrier_semaphore()
    for offset in range(1, n_tp):
        pl.semaphore_signal(
            barrier, inc=1, device_id=(c, peer(offset, 1)), device_id_type=MESH
        )
    greeted = n_tp - 1
    for near, distance in partners:
        greeted = greeted + jnp.where(near, 1, 0)

        @pl.when(near)
        def _():
            pl.semaphore_signal(
                barrier, inc=1, device_id=(c + distance, t), device_id_type=MESH
            )

    small = [
        pltpu.make_async_copy(start_hbm, start_buf, small_sem.at[0]),
        pltpu.make_async_copy(list_hbm, list_buf, small_sem.at[1]),
        pltpu.make_async_copy(slot_hbm, slot_buf, small_sem.at[2]),
    ]
    own_rows = pl.ds(pl.multiple_of(t * part, part), part)
    own_key_rows = pl.ds(pl.multiple_of(LIST * tokens + t * part, part), part)

    def cut(ref, size, which):
        return ref.at[:, :, pl.ds(pl.multiple_of(which * size, size), size)]

    own = [
        pltpu.make_async_copy(cut(k_hbm, kv_width, t), k_all.at[:, own_key_rows], own_sem.at[0]),
        pltpu.make_async_copy(cut(v_hbm, kv_width, t), v_all.at[:, own_key_rows], own_sem.at[1]),
        pltpu.make_async_copy(cut(q_hbm, width, t), q_all.at[:, own_rows], own_sem.at[2]),
    ]
    for copy in small + own:
        copy.start()
    pl.semaphore_wait(barrier, greeted)

    kv_copies = ([], [])
    q_copies = {}
    for which, (ref, dst) in enumerate(((k_hbm, k_all), (v_hbm, v_all))):
        for offset in ORDER:
            to = peer(offset, 1)
            copy = pltpu.make_async_remote_copy(
                src_ref=cut(ref, kv_width, to),
                dst_ref=dst.at[:, own_key_rows],
                send_sem=kv_send.at[which, offset],
                recv_sem=kv_recv.at[which, offset],
                device_id=(c, to),
                device_id_type=MESH,
            )
            copy.start()
            kv_copies[which].append(copy)
    for offset in ORDER:
        to = peer(offset, 1)
        q_copies[offset] = pltpu.make_async_remote_copy(
            src_ref=cut(q_hbm, width, to),
            dst_ref=q_all.at[:, own_rows],
            send_sem=q_send.at[offset],
            recv_sem=q_recv.at[offset],
            device_id=(c, to),
            device_id_type=MESH,
        )

    for offset in ORDER[:AHEAD]:
        q_copies[offset].start()

    for copy in small:
        copy.wait()
    upper = []
    for s in range(held):
        block_id = slot_buf[c * held + s]
        upper.append(jnp.where(block_id >= n_cp, 1, 0))
        named = jnp.int32(0)
        for entry in range(LIST):
            named = named + jnp.where(list_buf[s, entry] >= 0, tokens, 0)
        row = jnp.maximum(start_buf[s : s + 1, :] - block_id * tokens, -named)
        for at in range(0, tokens, 128):
            low_bound[s, at : at + 128, :] = jnp.broadcast_to(
                row[:, at : at + 128], (128, 128)
            ).T

    def far(which, src, dst, order, recv, distance):
        return pltpu.make_async_remote_copy(
            src_ref=src.at[which],
            dst_ref=dst.at[which],
            send_sem=far_send.at[order, which],
            recv_sem=recv.at[which],
            device_id=(c + distance, t),
            device_id_type=MESH,
        )

    low, high = stage.at[0], stage.at[1]
    box = [inbox.at[i] for i in range(4)]
    box_recv = [far_recv.at[i] for i in range(4)]
    first = [
        (c + 1 < n_cp, low, box[0], box_recv[0], 1),
        (c >= 1, high, box[2], box_recv[2], -1),
        (even & (c + 2 < n_cp) & ~climbs(c), low, box[1], box_recv[1], 2),
        (odd & (c >= 2) & ~descends(c), high, box[3], box_recv[3], -2),
        (climbs(c), low, relay, relay_recv, leg),
        (descends(c), high, relay, relay_recv, -leg),
    ]
    then = [
        (even & (c >= 2), box[0], box[1], box_recv[1], 1),
        (odd, box[2], box[3], box_recv[3], -1),
        (relays_low, relay, box[1], box_recv[1], rest),
        (relays_high, relay, box[3], box_recv[3], -rest),
    ]
    moves = [(order,) + move for order, move in enumerate(first + then)]

    def send(move, which):
        order, when, src, dst, recv, distance = move

        @pl.when(when)
        def _():
            far(which, src, dst, order, recv, distance).start()

    def arrive(when, which, dst, recv):
        @pl.when(when)
        def _():
            far(which, dst, dst, 0, recv, 0).wait_recv()

    for which, whole in enumerate((k_all, v_all)):
        own[which].wait()
        for copy in kv_copies[which]:
            copy.wait_recv()
        for place in range(held):
            slot = (upper[0] + place) % held
            stage[place, which] = whole[slot, pl.ds(LIST * tokens, tokens), :]
        for move in moves[: len(first)]:
            send(move, which)

    for offset in ORDER[AHEAD:]:
        q_copies[offset].start()

    @pl.when(c < 1)
    def _():
        inbox[0] = jnp.zeros(inbox.shape[1:], inbox.dtype)

    @pl.when(c < 2)
    def _():
        inbox[1] = jnp.zeros(inbox.shape[1:], inbox.dtype)

    @pl.when(c == n_cp - 1)
    def _():
        inbox[2] = stage[0]

    for which in range(2):
        arrive(even & (c >= 2), which, box[0], box_recv[0])
        arrive(odd & (c < n_cp - 1), which, box[2], box_recv[2])
        for move in moves[len(first) : len(first) + 2]:
            send(move, which)
        arrive(relays_low | relays_high, which, relay, relay_recv)
        for move in moves[len(first) + 2 :]:
            send(move, which)
    for which in range(2):
        arrive(odd, which, box[0], box_recv[0])
        arrive(c >= 2, which, box[1], box_recv[1])
        arrive(even, which, box[2], box_recv[2])
        arrive(c < n_cp - 1, which, box[3], box_recv[3])

    @pl.when(c == n_cp - 1)
    def _():
        inbox[3] = inbox[0]

    for s in range(held):
        for step in range(LIST):
            source = upper[s] * 2 + step
            rows = pl.ds((LIST - 1 - step) * tokens, tokens)
            k_all[s, rows, :] = inbox[source, 0]
            v_all[s, rows, :] = inbox[source, 1]

    def attend(s, start, size, half):
        rows = pl.ds(pl.multiple_of(start, size), size)
        begin = half * (tokens // 2)
        keys = pl.ds(pl.multiple_of(begin, tokens // 2), window)
        lane = lax.broadcasted_iota(jnp.int32, (size, 128), 1)
        sub = lax.broadcasted_iota(jnp.int32, (size, 128), 0)
        query = q_all[s, rows, :]
        query = jnp.concatenate(
            [query[:, h * HEAD_SIZE : (h + 1) * HEAD_SIZE] for h in range(group)], axis=0
        )
        scores = lax.dot_general(
            query, k_all[s, keys, :], (((1,), (1,)), ((), ())), preferred_element_type=jnp.float32
        )
        lowest = low_bound[s, rows, :]
        highest = sub + start
        visible = []
        for at in range(0, window, 128):
            key = lane + (begin + at - LIST * tokens)
            visible.append((key >= lowest) & (key <= highest))
        visible = jnp.concatenate(visible, axis=1)
        scores = scores.reshape(group, size, window)
        scores = jnp.where(visible[None], scores, neg_large)
        scores = scores.reshape(group * size, window)
        best = jnp.max(scores, axis=-1, keepdims=True)
        weights = jnp.exp2((scores - best) * SCALE)
        total = jnp.sum(weights, axis=-1, keepdims=True)
        mixed = jnp.dot(
            weights.astype(jnp.bfloat16), v_all[s, keys, :], preferred_element_type=jnp.float32
        )
        mixed = (mixed * (1.0 / total)).astype(jnp.bfloat16)
        for h in range(group):
            out_ref[s, rows, h * HEAD_SIZE : (h + 1) * HEAD_SIZE] = mixed[
                h * size : (h + 1) * size
            ]

    own[2].wait()
    for offsets in ((0, 1), (2, 3), (6, 7), (4,), (5,)):
        for offset in offsets:
            if offset:
                q_copies[offset].wait_recv()
        source_x = (x - offsets[0] // RUN + n_x) % n_x
        source = source_x * RUN if len(offsets) == RUN else peer(offsets[0], -1)
        for s in range(held):
            attend(s, source * part, len(offsets) * part, source_x // (n_x // 2))

    for copy in kv_copies[0] + kv_copies[1] + list(q_copies.values()):
        copy.wait_send()
    for order, when, src, dst, recv, distance in moves:

        @pl.when(when)
        def _():
            for which in range(2):
                far(which, src, dst, order, recv, distance).wait_send()


def on_device(n_cp, n_tp, *operands):
    query_rows, key_rows, _, _, source_lists, slot_block = operands
    held, part, all_width = query_rows.shape
    tokens = part * n_tp
    width = all_width // n_tp
    kv_width = key_rows.shape[2] // n_tp
    reach = (LIST + 1) * tokens
    bf16, i32 = jnp.bfloat16, jnp.int32
    dma = pltpu.SemaphoreType.DMA
    return pl.pallas_call(
        functools.partial(kernel, n_cp, n_tp),
        out_shape=pltpu.VMEM((held, tokens, width), bf16),
        in_specs=[pl.BlockSpec(memory_space=pltpu.HBM)] * 6,
        out_specs=pl.BlockSpec(memory_space=pltpu.VMEM),
        scratch_shapes=[
            pltpu.VMEM((held, tokens, width), bf16),
            pltpu.VMEM((held, reach, kv_width), bf16),
            pltpu.VMEM((held, reach, kv_width), bf16),
            pltpu.VMEM((2, 2, tokens, kv_width), bf16),
            pltpu.VMEM((4, 2, tokens, kv_width), bf16),
            pltpu.VMEM((2, tokens, kv_width), bf16),
            pltpu.VMEM((held, tokens), i32),
            pltpu.VMEM((held, tokens, 128), i32),
            pltpu.SMEM(source_lists.shape, i32),
            pltpu.SMEM(slot_block.shape, i32),
            dma((3,)),
            dma((3,)),
            dma((2, n_tp)),
            dma((2, n_tp)),
            dma((n_tp,)),
            dma((n_tp,)),
            dma((10, 2)),
            dma((4, 2)),
            dma((2,)),
        ],
        compiler_params=pltpu.CompilerParams(
            collective_id=0, has_side_effects=True, vmem_limit_bytes=40 * 1024 * 1024
        ),
        name="attention",
    )(*(pltpu.with_memory_space_constraint(operand, pltpu.HBM) for operand in operands))


def solution(mesh):
    in_specs = (
        P("cp", "tp", None),
        P("cp", "tp", None),
        P("cp", "tp", None),
        P("cp", None),
        P("cp", None),
        P(),
    )
    out_specs = P("cp", None, "tp")
    return jax.shard_map(
        functools.partial(on_device, mesh.shape["cp"], mesh.shape["tp"]),
        mesh=mesh,
        in_specs=in_specs,
        out_specs=out_specs,
        check_vma=False,
    )
```

```python
import functools

import jax
import jax.numpy as jnp
from jax import lax
from jax.experimental import pallas as pl
from jax.experimental.pallas import tpu as pltpu
from jax.sharding import PartitionSpec as P

QUERY_HEAD_COUNT = 64
KEY_VALUE_HEADS = 8
HEAD_SIZE = 128
LIST = 2
MESH = pl.DeviceIdType.MESH

neg_large = -1e30
SCALE = HEAD_SIZE ** (-0.5) * 1.4426950408889634
RUN = 2
ORDER = (1, 2, 6, 3, 7, 4, 5)
AHEAD = 3
SCHEDULE = (
    ("a", (0, 1)),
    ("a", (2, 3)),
    ("hand", ()),
    ("a", (6, 7)),
    ("keys", ()),
    ("b", (0, 1)),
    ("b", (2, 3)),
    ("b", (6, 7)),
    ("a", (4,)),
    ("b", (4,)),
    ("a", (5,)),
    ("b", (5,)),
)
GROUP = 16
ASIDE = ((14, 0, 16, -14), (14, 1, 14, -12), (15, 1, 3, -2))


def kernel(
    n_cp,
    n_tp,
    q_hbm,
    k_hbm,
    v_hbm,
    start_hbm,
    list_hbm,
    slot_hbm,
    out_ref,
    q_all,
    k_all,
    v_all,
    k_raw,
    v_raw,
    k_cut,
    v_cut,
    relay,
    done,
    start_buf,
    low_bound,
    list_buf,
    slot_buf,
    small_sem,
    raw_sem,
    own_sem,
    kv_send,
    kv_recv,
    q_send,
    q_recv,
    far_send,
    far_recv,
    relay_recv,
    answer,
):
    held, part, _ = q_hbm.shape
    tokens = part * n_tp
    width = q_hbm.shape[2] // n_tp
    kv_width = k_hbm.shape[2] // n_tp
    group = width // HEAD_SIZE
    window = LIST * tokens + tokens // 2
    c = lax.axis_index("cp")
    t = lax.axis_index("tp")
    n_x = n_tp // RUN
    x, z = t // RUN, t % RUN

    def peer(offset, sign):
        dx, dz = offset // RUN, offset % RUN
        return ((x + sign * dx + n_x) % n_x) * RUN + (z + sign * dz + RUN) % RUN

    def climbs(who, place):
        return (who >= 0) & (who + GROUP < n_cp) & ((who + 2 * GROUP) % GROUP == place)

    def descends(who, place):
        return (who >= GROUP) & (who < n_cp) & (who % GROUP == GROUP - 1 - place)

    even = c % 2 == 0
    odd = c % 2 == 1

    pairs = []

    def pair(holds, distance):
        if distance > 0:
            pairs.append((holds(c), holds(c - distance), distance, True))
        else:
            pairs.append((holds(c - distance), holds(c), -distance, False))
        return len(pairs) - 1

    near = [pair(lambda who, d=d: (who >= 0) & (who + d < n_cp), d) for d in (1, 2)]
    outward, onward = {}, {}
    for place, which, leg, rest in ASIDE:
        for goes, way in ((climbs, 1), (descends, -1)):
            go = functools.partial(goes, place=place)
            outward[place, which, way] = pair(go, way * leg)
            onward[place, which, way] = pair(lambda who, go=go, leg=way * leg: go(who - leg), way * rest)

    barrier = pltpu.get_barrier_semaphore()
    for offset in range(1, n_tp):
        pl.semaphore_signal(
            barrier, inc=1, device_id=(c, peer(offset, 1)), device_id_type=MESH
        )
    greeted = n_tp - 1
    for is_lower, is_upper, distance, _ in pairs:
        greeted = greeted + jnp.where(is_upper, 1, 0)

        @pl.when(is_lower)
        def _():
            pl.semaphore_signal(
                barrier, inc=1, device_id=(c + distance, t), device_id_type=MESH
            )

    def answered(number):
        @pl.when(pairs[number][0])
        def _():
            pl.semaphore_wait(answer.at[number], 1)

    small = [
        pltpu.make_async_copy(slot_hbm, slot_buf, small_sem.at[0]),
        pltpu.make_async_copy(start_hbm, start_buf, small_sem.at[1]),
        pltpu.make_async_copy(list_hbm, list_buf, small_sem.at[2]),
    ]
    raw = [
        pltpu.make_async_copy(k_hbm, k_raw, raw_sem.at[0]),
        pltpu.make_async_copy(v_hbm, v_raw, raw_sem.at[1]),
    ]
    own_rows = pl.ds(pl.multiple_of(t * part, part), part)
    own_key_rows = pl.ds(pl.multiple_of(LIST * tokens + t * part, part), part)

    def cut(ref, size, which):
        return ref.at[:, :, pl.ds(pl.multiple_of(which * size, size), size)]

    own = [
        pltpu.make_async_copy(cut(k_cut, kv_width, t), k_all.at[:, own_key_rows], own_sem.at[0]),
        pltpu.make_async_copy(cut(v_cut, kv_width, t), v_all.at[:, own_key_rows], own_sem.at[1]),
        pltpu.make_async_copy(cut(q_hbm, width, t), q_all.at[:, own_rows], own_sem.at[2]),
    ]
    for copy in small[:1] + raw + small[1:] + own[2:]:
        copy.start()

    small[0].wait()
    block_ids = [slot_buf[c * held + s] for s in range(held)]
    swapped = block_ids[0] >= n_cp

    def in_place(place, of_slot):
        return jnp.where(swapped, of_slot(1 - place), of_slot(place))

    for which, (ref, dst) in enumerate(((k_raw, k_cut), (v_raw, v_cut))):
        raw[which].wait()
        for place in range(held):
            dst[place] = in_place(place, lambda s: ref[s])
        own[which].start()
    pl.semaphore_wait(barrier, greeted)

    kv_copies = ([], [])
    q_copies = {}
    for which, (ref, dst) in enumerate(((k_cut, k_all), (v_cut, v_all))):
        for offset in ORDER:
            to = peer(offset, 1)
            copy = pltpu.make_async_remote_copy(
                src_ref=cut(ref, kv_width, to),
                dst_ref=dst.at[:, own_key_rows],
                send_sem=kv_send.at[which, offset],
                recv_sem=kv_recv.at[which, offset],
                device_id=(c, to),
                device_id_type=MESH,
            )
            copy.start()
            kv_copies[which].append(copy)
    for offset in ORDER:
        to = peer(offset, 1)
        q_copies[offset] = pltpu.make_async_remote_copy(
            src_ref=cut(q_hbm, width, to),
            dst_ref=q_all.at[:, own_rows],
            send_sem=q_send.at[offset],
            recv_sem=q_recv.at[offset],
            device_id=(c, to),
            device_id_type=MESH,
        )
    for offset in ORDER[:AHEAD]:
        q_copies[offset].start()

    for number, (is_lower, is_upper, distance, sends) in enumerate(pairs):

        @pl.when(is_upper & sends)
        def _():
            pl.semaphore_signal(
                answer.at[number], inc=1, device_id=(c - distance, t), device_id_type=MESH
            )

    for copy in small[1:]:
        copy.wait()

    def lowest_of(s):
        named = jnp.int32(0)
        for entry in range(LIST):
            named = named + jnp.where(list_buf[s, entry] >= 0, tokens, 0)
        return jnp.maximum(start_buf[s : s + 1, :] - block_ids[s] * tokens, -named)

    for place in range(held):
        row = in_place(place, lowest_of)
        for at in range(0, tokens, 128):
            low_bound[place, at : at + 128, :] = jnp.broadcast_to(
                row[:, at : at + 128], (128, 128)
            ).T

    def segment(place, below):
        rows = pl.ds((LIST - below) * tokens, tokens)
        return [k_all.at[place, rows], v_all.at[place, rows]]

    def far(which, src, dst, order, recv, distance):
        return pltpu.make_async_remote_copy(
            src_ref=src[which],
            dst_ref=dst[which],
            send_sem=far_send.at[order, which],
            recv_sem=recv[which],
            device_id=(c + distance, t),
            device_id_type=MESH,
        )

    low, high = segment(0, 0), segment(1, 0)
    low_1, low_2, high_1, high_2 = segment(0, 1), segment(0, 2), segment(1, 1), segment(1, 2)
    low_1_in, low_2_in, high_1_in, high_2_in = [
        [far_recv.at[i, which] for which in range(2)] for i in range(4)
    ]
    aside, aside_in = [relay.at[0], relay.at[1]], [relay_recv.at[0], relay_recv.at[1]]
    last = c == n_cp - 1
    late = (c % GROUP == 0) | ((c % GROUP == GROUP - 1) & ~last)
    hand_low, hand_high = even & (c >= 2), odd
    both, edge = (0, 1), GROUP - 1
    first = [
        ((0,), c + 1 < n_cp, low, low_1, low_1_in, 1),
        ((1,), (c + 1 < n_cp) & ~climbs(c, edge), low, low_1, low_1_in, 1),
        ((0,), c >= 1, high, high_1, high_1_in, -1),
        ((1,), (c >= 1) & ~descends(c, edge), high, high_1, high_1_in, -1),
        (both, even & (c + 2 < n_cp) & ~climbs(c, edge - 1), low, low_2, low_2_in, 2),
        (both, odd & (c >= 2) & ~descends(c, edge - 1), high, high_2, high_2_in, -2),
    ]
    passed = []
    for place, which, leg, rest in ASIDE:
        first += [
            ((which,), climbs(c, place), low, aside, aside_in, leg),
            ((which,), descends(c, place), high, aside, aside_in, -leg),
        ]
        to_low, to_high = (low_1, high_1) if place == edge else (low_2, high_2)
        in_low, in_high = (low_1_in, high_1_in) if place == edge else (low_2_in, high_2_in)
        passed += [
            ((which,), climbs(c - leg, place), aside, to_low, in_low, rest),
            ((which,), descends(c + leg, place), aside, to_high, in_high, -rest),
        ]
    handed = [
        (both, hand_low, low_1, low_2, low_2_in, 1),
        (both, hand_high, high_1, high_2, high_2_in, -1),
    ]
    moves = [(order,) + move for order, move in enumerate(first + passed + handed)]
    ways = [key + (way,) for key in ((a[0], a[1]) for a in ASIDE) for way in (1, -1)]
    waits = {len(first) - len(ways) + i: outward[key] for i, key in enumerate(ways)}
    waits.update({len(first) + i: onward[key] for i, key in enumerate(ways)})
    first, passed, handed = moves[: len(first)], moves[len(first) : -2], moves[-2:]

    def send(move, which, also=True):
        order, whiches, when, src, dst, recv, distance = move
        if which in whiches:
            if order in waits and distance > 0:
                answered(waits[order])

            @pl.when(when & also)
            def _():
                far(which, src, dst, order, recv, distance).start()

    def arrive(when, which, dst, recv):
        @pl.when(when)
        def _():
            far(which, dst, dst, 0, recv, 0).wait_recv()

    def hand_on(which, also):
        arrive(hand_low & also, which, low_1, low_1_in)
        arrive(hand_high & ~last & also, which, high_1, high_1_in)
        for move in handed:
            send(move, which, also)

    for which in range(2):
        own[which].wait()
        for copy in kv_copies[which]:
            copy.wait_recv()
        for move in first:
            if move[-1] < 0:
                send(move, which)
        if which == 0:
            for number in near:
                answered(number)
        for move in first:
            if move[-1] > 0:
                send(move, which)
    for offset in ORDER[AHEAD:]:
        q_copies[offset].start()

    for which in range(2):

        @pl.when(c < 1)
        def _():
            low_1[which][...] = jnp.zeros((tokens, kv_width), k_all.dtype)

        @pl.when(c < 2)
        def _():
            low_2[which][...] = jnp.zeros((tokens, kv_width), k_all.dtype)

        @pl.when(last)
        def _():
            high_1[which][...] = low[which][...]

    for which in range(2):
        hand_on(which, ~late)
        for move in passed:
            if which in move[1]:
                arrive(move[2], which, aside, aside_in)
            send(move, which)

    place_a = jnp.where(c % GROUP < 2, 1, 0)
    place_b = 1 - place_a

    def keys_in(place):
        for which in range(2):
            arrive((place == 0) & odd, which, low_1, low_1_in)
            arrive((place == 0) & (c >= 2), which, low_2, low_2_in)
            arrive((place == 1) & even, which, high_1, high_1_in)
            arrive((place == 1) & ~last, which, high_2, high_2_in)

            @pl.when((place == 1) & last)
            def _():
                high_2[which][...] = low_1[which][...]

    def attend(place, start, size, half):
        rows = pl.ds(pl.multiple_of(start, size), size)
        slot = jnp.where(swapped, 1 - place, place)
        begin = half * (tokens // 2)
        keys = pl.ds(pl.multiple_of(begin, tokens // 2), window)
        lane = lax.broadcasted_iota(jnp.int32, (size, 128), 1)
        sub = lax.broadcasted_iota(jnp.int32, (size, 128), 0)
        query = jnp.where(slot == 0, q_all[0, rows, :], q_all[1, rows, :])
        query = jnp.concatenate(
            [query[:, h * HEAD_SIZE : (h + 1) * HEAD_SIZE] for h in range(group)], axis=0
        )
        scores = lax.dot_general(
            query, k_all[place, keys, :], (((1,), (1,)), ((), ())), preferred_element_type=jnp.float32
        )
        lowest = low_bound[place, rows, :]
        highest = sub + start
        visible = []
        for at in range(0, window, 128):
            key = lane + (begin + at - LIST * tokens)
            visible.append((key >= lowest) & (key <= highest))
        visible = jnp.concatenate(visible, axis=1)
        scores = scores.reshape(group, size, window)
        scores = jnp.where(visible[None], scores, neg_large)
        scores = scores.reshape(group * size, window)
        best = jnp.max(scores, axis=-1, keepdims=True)
        weights = jnp.exp2((scores - best) * SCALE)
        total = jnp.sum(weights, axis=-1, keepdims=True)
        mixed = jnp.dot(
            weights.astype(jnp.bfloat16), v_all[place, keys, :], preferred_element_type=jnp.float32
        )
        mixed = (mixed * (1.0 / total)).astype(jnp.bfloat16)
        return jnp.concatenate([mixed[h * size : (h + 1) * size] for h in range(group)], axis=1)

    def part_of(offsets):
        source_x = (x - offsets[0] // RUN + n_x) % n_x
        source = source_x * RUN if len(offsets) == RUN else peer(offsets[0], -1)
        return source * part, len(offsets) * part, source_x // (n_x // 2)

    own[2].wait()
    keys_in(place_a)
    arrived = {0}
    for turn, offsets in SCHEDULE:
        if turn == "hand":
            for which in range(2):
                hand_on(which, late)
            continue
        if turn == "keys":
            keys_in(place_b)
            continue
        for offset in offsets:
            if offset not in arrived:
                arrived.add(offset)
                q_copies[offset].wait_recv()
        start, size, half = part_of(offsets)
        rows = pl.ds(pl.multiple_of(start, size), size)
        if turn == "a":
            done[rows, :] = attend(place_a, start, size, half)
        else:
            result_a, result_b = done[rows, :], attend(place_b, start, size, half)
            b_is_0 = swapped == (place_b == 1)
            out_ref[0, rows, :] = jnp.where(b_is_0, result_b, result_a)
            out_ref[1, rows, :] = jnp.where(b_is_0, result_a, result_b)

    for copy in kv_copies[0] + kv_copies[1] + list(q_copies.values()):
        copy.wait_send()
    for order, whiches, when, src, dst, recv, distance in moves:

        @pl.when(when)
        def _():
            for which in whiches:
                far(which, src, dst, order, recv, distance).wait_send()


def on_device(n_cp, n_tp, *operands):
    query_rows, key_rows, _, _, source_lists, slot_block = operands
    held, part, all_width = query_rows.shape
    tokens = part * n_tp
    width = all_width // n_tp
    kv_width = key_rows.shape[2] // n_tp
    reach = (LIST + 1) * tokens
    bf16, i32 = jnp.bfloat16, jnp.int32
    dma = pltpu.SemaphoreType.DMA
    return pl.pallas_call(
        functools.partial(kernel, n_cp, n_tp),
        out_shape=pltpu.VMEM((held, tokens, width), bf16),
        in_specs=[pl.BlockSpec(memory_space=pltpu.HBM)] * 6,
        out_specs=pl.BlockSpec(memory_space=pltpu.VMEM),
        scratch_shapes=[
            pltpu.VMEM((held, tokens, width), bf16),
            pltpu.VMEM((held, reach, kv_width), bf16),
            pltpu.VMEM((held, reach, kv_width), bf16),
            pltpu.VMEM(key_rows.shape, bf16),
            pltpu.VMEM(key_rows.shape, bf16),
            pltpu.VMEM(key_rows.shape, bf16),
            pltpu.VMEM(key_rows.shape, bf16),
            pltpu.VMEM((2, tokens, kv_width), bf16),
            pltpu.VMEM((tokens, width), bf16),
            pltpu.VMEM((held, tokens), i32),
            pltpu.VMEM((held, tokens, 128), i32),
            pltpu.SMEM(source_lists.shape, i32),
            pltpu.SMEM(slot_block.shape, i32),
            dma((3,)),
            dma((2,)),
            dma((3,)),
            dma((2, n_tp)),
            dma((2, n_tp)),
            dma((n_tp,)),
            dma((n_tp,)),
            dma((8 + 4 * len(ASIDE), 2)),
            dma((4, 2)),
            dma((2,)),
            pltpu.SemaphoreType.REGULAR((2 + 4 * len(ASIDE),)),
        ],
        compiler_params=pltpu.CompilerParams(
            collective_id=0, has_side_effects=True, vmem_limit_bytes=40 * 1024 * 1024
        ),
        name="attention",
    )(*(pltpu.with_memory_space_constraint(operand, pltpu.HBM) for operand in operands))


def solution(mesh):
    in_specs = (
        P("cp", "tp", None),
        P("cp", "tp", None),
        P("cp", "tp", None),
        P("cp", None),
        P("cp", None),
        P(),
    )
    out_specs = P("cp", None, "tp")
    return jax.shard_map(
        functools.partial(on_device, mesh.shape["cp"], mesh.shape["tp"]),
        mesh=mesh,
        in_specs=in_specs,
        out_specs=out_specs,
        check_vma=False,
    )
```

```python
import functools

import jax
import jax.numpy as jnp
from jax import lax
from jax.experimental import pallas as pl
from jax.experimental.pallas import tpu as pltpu
from jax.sharding import PartitionSpec as P

QUERY_HEAD_COUNT = 64
KEY_VALUE_HEADS = 8
HEAD_SIZE = 128
LIST = 2
MESH = pl.DeviceIdType.MESH

neg_large = -1e30
SCALE = HEAD_SIZE ** (-0.5) * 1.4426950408889634
RUN = 2
ORDER = (1, 2, 6, 3, 7, 4, 5)
AHEAD = 3
SCHEDULE = (
    (("a", (0, 1)), ("a", (2, 3))),
    "keys",
    (("b", (0, 1)), ("b", (2, 3))),
    (("a", (6, 7)), ("b", (6, 7))),
    (("a", (4,)), ("b", (4,))),
    (("a", (5,)), ("b", (5,))),
)
GROUP = 16
ASIDE = ((14, 0, 16, -14), (14, 1, 14, -12), (15, 0, 1, 0), (15, 1, 3, -2))


def kernel(
    n_cp,
    n_tp,
    q_hbm,
    k_hbm,
    v_hbm,
    start_hbm,
    list_hbm,
    slot_hbm,
    out_ref,
    q_all,
    k_all,
    v_all,
    k_raw,
    v_raw,
    k_cut,
    v_cut,
    relay,
    done,
    start_buf,
    low_bound,
    list_buf,
    slot_buf,
    small_sem,
    raw_sem,
    own_sem,
    kv_send,
    kv_recv,
    q_send,
    q_recv,
    far_send,
    far_recv,
    relay_recv,
    cross_send,
    answer,
):
    held, part, _ = q_hbm.shape
    tokens = part * n_tp
    width = q_hbm.shape[2] // n_tp
    kv_width = k_hbm.shape[2] // n_tp
    group = width // HEAD_SIZE
    window = LIST * tokens + tokens // 2
    c = lax.axis_index("cp")
    t = lax.axis_index("tp")
    n_x = n_tp // RUN
    x, z = t // RUN, t % RUN

    def peer(offset, sign):
        dx, dz = offset // RUN, offset % RUN
        return ((x + sign * dx + n_x) % n_x) * RUN + (z + sign * dz + RUN) % RUN

    def climbs(who, place):
        return (who >= 0) & (who + GROUP < n_cp) & ((who + 2 * GROUP) % GROUP == place)

    def descends(who, place):
        return (who >= GROUP) & (who < n_cp) & (who % GROUP == GROUP - 1 - place)

    even = c % 2 == 0
    odd = c % 2 == 1

    pairs = []

    def pair(holds, distance, whole=False):
        if distance > 0:
            pairs.append((holds(c), holds(c - distance), distance, True, False))
        else:
            pairs.append((holds(c - distance), holds(c), -distance, False, whole))
        return len(pairs) - 1

    near = [pair(lambda who, d=d: (who >= 0) & (who + d < n_cp), d) for d in (1, 2)]
    outward, onward = {}, {}
    for place, which, leg, rest in ASIDE:
        for goes, way in ((climbs, 1), (descends, -1)):
            go = functools.partial(goes, place=place)
            outward[place, which, way] = pair(go, way * leg, True)
            if rest:
                onward[place, which, way] = pair(lambda who, go=go, leg=way * leg: go(who - leg), way * rest)

    barrier = pltpu.get_barrier_semaphore()
    for offset in range(1, n_tp):
        pl.semaphore_signal(
            barrier, inc=1, device_id=(c, peer(offset, 1)), device_id_type=MESH
        )
    greeted = n_tp - 1

    for is_lower, is_upper, distance, _, whole in pairs:
        greeted = greeted + jnp.where(is_upper, n_tp if whole else 1, 0)

        @pl.when(is_lower)
        def _():
            for to in range(n_tp) if whole else (t,):
                pl.semaphore_signal(
                    barrier, inc=1, device_id=(c + distance, to), device_id_type=MESH
                )

    def answered(number):
        @pl.when(pairs[number][0])
        def _():
            pl.semaphore_wait(answer.at[number], 1)

    small = [
        pltpu.make_async_copy(slot_hbm, slot_buf, small_sem.at[0]),
        pltpu.make_async_copy(start_hbm, start_buf, small_sem.at[1]),
        pltpu.make_async_copy(list_hbm, list_buf, small_sem.at[2]),
    ]
    raw = [
        pltpu.make_async_copy(k_hbm, k_raw, raw_sem.at[0]),
        pltpu.make_async_copy(v_hbm, v_raw, raw_sem.at[1]),
    ]
    own_rows = pl.ds(pl.multiple_of(t * part, part), part)
    own_key_rows = pl.ds(pl.multiple_of(LIST * tokens + t * part, part), part)

    def cut(ref, size, which):
        return ref.at[:, :, pl.ds(pl.multiple_of(which * size, size), size)]

    own = [
        pltpu.make_async_copy(cut(k_cut, kv_width, t), k_all.at[:, own_key_rows], own_sem.at[0]),
        pltpu.make_async_copy(cut(v_cut, kv_width, t), v_all.at[:, own_key_rows], own_sem.at[1]),
        pltpu.make_async_copy(cut(q_hbm, width, t), q_all.at[:, own_rows], own_sem.at[2]),
    ]
    for copy in small[:1] + raw + small[1:] + own[2:]:
        copy.start()

    small[0].wait()
    block_ids = [slot_buf[c * held + s] for s in range(held)]
    swapped = block_ids[0] >= n_cp

    def in_place(place, of_slot):
        return jnp.where(swapped, of_slot(1 - place), of_slot(place))

    for which, (ref, dst) in enumerate(((k_raw, k_cut), (v_raw, v_cut))):
        raw[which].wait()
        for place in range(held):
            dst[place] = in_place(place, lambda s: ref[s])
        own[which].start()
    pl.semaphore_wait(barrier, greeted)
    for number, (_, is_upper, distance, sends, _) in enumerate(pairs):

        @pl.when(is_upper & sends)
        def _():
            pl.semaphore_signal(
                answer.at[number], inc=1, device_id=(c - distance, t), device_id_type=MESH
            )

    kv_copies = ([], [])
    q_copies = {}
    for which, (ref, dst) in enumerate(((k_cut, k_all), (v_cut, v_all))):
        for offset in ORDER:
            to = peer(offset, 1)
            copy = pltpu.make_async_remote_copy(
                src_ref=cut(ref, kv_width, to),
                dst_ref=dst.at[:, own_key_rows],
                send_sem=kv_send.at[which, offset],
                recv_sem=kv_recv.at[which, offset],
                device_id=(c, to),
                device_id_type=MESH,
            )
            copy.start()
            kv_copies[which].append(copy)
    def segment(place, below):
        rows = pl.ds((LIST - below) * tokens, tokens)
        return [k_all.at[place, rows], v_all.at[place, rows]]

    low, high = segment(0, 0), segment(1, 0)
    low_1, low_2, high_1, high_2 = segment(0, 1), segment(0, 2), segment(1, 1), segment(1, 2)
    low_1_in, low_2_in, high_1_in, high_2_in = [
        [far_recv.at[i, which] for which in range(2)] for i in range(4)
    ]
    aside, aside_in = [relay.at[0], relay.at[1]], [relay_recv.at[0], relay_recv.at[1]]

    edge = GROUP - 1
    crossing = {1: [], -1: []}
    for number, (place, which, leg, rest) in enumerate(ASIDE):
        for goes, way, side in ((climbs, 1, 0), (descends, -1, 1)):
            dst, recv = aside[which], aside_in[which]
            if not rest:
                dst, recv = ((low_1, low_1_in), (high_1, high_1_in))[side]
                dst, recv = dst[which], recv[which]
            copies = [
                pltpu.make_async_remote_copy(
                    src_ref=(k_cut, v_cut)[which].at[side, :, pl.ds(to * kv_width, kv_width)],
                    dst_ref=dst.at[own_rows],
                    send_sem=cross_send.at[number, to],
                    recv_sem=recv,
                    device_id=(c + way * leg, to),
                    device_id_type=MESH,
                )
                for to in range(n_tp)
            ]
            crossing[way].append((goes(c, place), (place, which, way), copies))

    def cross(way):
        for when, key, copies in crossing[way]:
            if way > 0:
                answered(outward[key])

            @pl.when(when)
            def _():
                for copy in copies:
                    copy.start()

    cross(-1)
    for offset in ORDER:
        to = peer(offset, 1)
        q_copies[offset] = pltpu.make_async_remote_copy(
            src_ref=cut(q_hbm, width, to),
            dst_ref=q_all.at[:, own_rows],
            send_sem=q_send.at[offset],
            recv_sem=q_recv.at[offset],
            device_id=(c, to),
            device_id_type=MESH,
        )

    crosses_up = (c + GROUP < n_cp) & (c % GROUP >= edge - 1)
    for offset in ORDER[:AHEAD]:
        q_copies[offset].start()

    @pl.when(~crosses_up)
    def _():
        for offset in ORDER[AHEAD:]:
            q_copies[offset].start()

    cross(1)

    @pl.when(crosses_up)
    def _():
        for offset in ORDER[AHEAD:]:
            q_copies[offset].start()

    for copy in small[1:]:
        copy.wait()

    def lowest_of(s):
        named = jnp.int32(0)
        for entry in range(LIST):
            named = named + jnp.where(list_buf[s, entry] >= 0, tokens, 0)
        return jnp.maximum(start_buf[s : s + 1, :] - block_ids[s] * tokens, -named)

    for place in range(held):
        row = in_place(place, lowest_of)
        for at in range(0, tokens, 128):
            low_bound[place, at : at + 128, :] = jnp.broadcast_to(
                row[:, at : at + 128], (128, 128)
            ).T

    def far(which, src, dst, order, recv, distance):
        return pltpu.make_async_remote_copy(
            src_ref=src[which],
            dst_ref=dst[which],
            send_sem=far_send.at[order, which],
            recv_sem=recv[which],
            device_id=(c + distance, t),
            device_id_type=MESH,
        )

    last = c == n_cp - 1
    hand_low, hand_high = even & (c >= 2), odd
    both = (0, 1)
    first = [
        (both, (c + 1 < n_cp) & ~climbs(c, edge), low, low_1, low_1_in, 1),
        (both, (c >= 1) & ~descends(c, edge), high, high_1, high_1_in, -1),
        (both, even & (c + 2 < n_cp) & ~climbs(c, edge - 1), low, low_2, low_2_in, 2),
        (both, odd & (c >= 2) & ~descends(c, edge - 1), high, high_2, high_2_in, -2),
    ]
    passed = []
    for place, which, leg, rest in ASIDE:
        if rest:
            to_low, to_high = (low_1, high_1) if place == edge else (low_2, high_2)
            in_low, in_high = (low_1_in, high_1_in) if place == edge else (low_2_in, high_2_in)
            passed += [
                ((which,), climbs(c - leg, place), aside, to_low, in_low, rest),
                ((which,), descends(c + leg, place), aside, to_high, in_high, -rest),
            ]
    handed = [
        (both, hand_low, low_1, low_2, low_2_in, 1),
        (both, hand_high, high_1, high_2, high_2_in, -1),
    ]
    moves = [(order,) + move for order, move in enumerate(first + passed + handed)]
    ways = [(place, which, way) for place, which, _, rest in ASIDE if rest for way in (1, -1)]
    waits = {len(first) + i: onward[key] for i, key in enumerate(ways)}
    first, passed, handed = moves[: len(first)], moves[len(first) : -2], moves[-2:]

    def send(move, which):
        order, whiches, when, src, dst, recv, distance = move
        if which in whiches:
            if order in waits and distance > 0:
                answered(waits[order])

            @pl.when(when)
            def _():
                far(which, src, dst, order, recv, distance).start()

    def arrive(when, which, dst, recv):
        @pl.when(when)
        def _():
            far(which, dst, dst, 0, recv, 0).wait_recv()

    def hand_on(which):
        arrive(hand_low, which, low_1, low_1_in)
        arrive(hand_high & ~last, which, high_1, high_1_in)
        for move in handed:
            send(move, which)

    for which in range(2):
        own[which].wait()
        for copy in kv_copies[which]:
            copy.wait_recv()
        for move in first:
            if move[-1] < 0:
                send(move, which)
        if which == 0:
            for number in near:
                answered(number)
        for move in first:
            if move[-1] > 0:
                send(move, which)
    for which in range(2):

        @pl.when(c < 1)
        def _():
            low_1[which][...] = jnp.zeros((tokens, kv_width), k_all.dtype)

        @pl.when(c < 2)
        def _():
            low_2[which][...] = jnp.zeros((tokens, kv_width), k_all.dtype)

        @pl.when(last)
        def _():
            high_1[which][...] = low[which][...]

    for which in range(2):
        for move in passed:
            if which in move[1]:
                arrive(move[2], which, aside, aside_in)
            send(move, which)
    for which in range(2):
        hand_on(which)

    place_a = jnp.where(c % GROUP < 2, 1, 0)
    place_b = 1 - place_a

    def keys_in(place):
        for which in range(2):
            arrive((place == 0) & odd, which, low_1, low_1_in)
            arrive((place == 0) & (c >= 2), which, low_2, low_2_in)
            arrive((place == 1) & even, which, high_1, high_1_in)
            arrive((place == 1) & ~last, which, high_2, high_2_in)

            @pl.when((place == 1) & last)
            def _():
                high_2[which][...] = low_1[which][...]

    def attend(place, start, size, half):
        rows = pl.ds(pl.multiple_of(start, size), size)
        slot = jnp.where(swapped, 1 - place, place)
        begin = half * (tokens // 2)
        keys = pl.ds(pl.multiple_of(begin, tokens // 2), window)
        lane = lax.broadcasted_iota(jnp.int32, (size, 128), 1)
        sub = lax.broadcasted_iota(jnp.int32, (size, 128), 0)
        query = jnp.where(slot == 0, q_all[0, rows, :], q_all[1, rows, :])
        query = jnp.concatenate(
            [query[:, h * HEAD_SIZE : (h + 1) * HEAD_SIZE] for h in range(group)], axis=0
        )
        scores = lax.dot_general(
            query, k_all[place, keys, :], (((1,), (1,)), ((), ())), preferred_element_type=jnp.float32
        )
        lowest = low_bound[place, rows, :]
        highest = sub + start
        visible = []
        for at in range(0, window, 128):
            key = lane + (begin + at - LIST * tokens)
            visible.append((key >= lowest) & (key <= highest))
        visible = jnp.concatenate(visible, axis=1)
        scores = scores.reshape(group, size, window)
        scores = jnp.where(visible[None], scores, neg_large)
        scores = scores.reshape(group * size, window)
        best = jnp.max(scores, axis=-1, keepdims=True)
        weights = jnp.exp2((scores - best) * SCALE)
        total = jnp.sum(weights, axis=-1, keepdims=True)
        mixed = jnp.dot(
            weights.astype(jnp.bfloat16), v_all[place, keys, :], preferred_element_type=jnp.float32
        )
        mixed = (mixed * (1.0 / total)).astype(jnp.bfloat16)
        return jnp.concatenate([mixed[h * size : (h + 1) * size] for h in range(group)], axis=1)

    def part_of(offsets):
        source_x = (x - offsets[0] // RUN + n_x) % n_x
        source = source_x * RUN if len(offsets) == RUN else peer(offsets[0], -1)
        return source * part, len(offsets) * part, source_x // (n_x // 2)

    own[2].wait()
    keys_in(place_a)
    arrived = {0}
    for step in SCHEDULE:
        if step == "keys":
            keys_in(place_b)
            continue
        for _, offsets in step:
            for offset in offsets:
                if offset not in arrived:
                    arrived.add(offset)
                    q_copies[offset].wait_recv()
        results = {}
        for turn, offsets in step:
            place = place_a if turn == "a" else place_b
            start, size, half = part_of(offsets)
            results[turn, offsets] = start, size, attend(place, start, size, half)
        for (turn, offsets), (start, size, result) in results.items():
            rows = pl.ds(pl.multiple_of(start, size), size)
            if turn == "b":
                result_a = results["a", offsets][2] if ("a", offsets) in results else done[rows, :]
                b_is_0 = swapped == (place_b == 1)
                out_ref[0, rows, :] = jnp.where(b_is_0, result, result_a)
                out_ref[1, rows, :] = jnp.where(b_is_0, result_a, result)
            elif ("b", offsets) not in results:
                done[rows, :] = result

    for copy in kv_copies[0] + kv_copies[1] + list(q_copies.values()):
        copy.wait_send()
    for when, _, copies in crossing[1] + crossing[-1]:

        @pl.when(when)
        def _():
            for copy in copies:
                copy.wait_send()

    for order, whiches, when, src, dst, recv, distance in moves:

        @pl.when(when)
        def _():
            for which in whiches:
                far(which, src, dst, order, recv, distance).wait_send()


def on_device(n_cp, n_tp, *operands):
    query_rows, key_rows, _, _, source_lists, slot_block = operands
    held, part, all_width = query_rows.shape
    tokens = part * n_tp
    width = all_width // n_tp
    kv_width = key_rows.shape[2] // n_tp
    reach = (LIST + 1) * tokens
    bf16, i32 = jnp.bfloat16, jnp.int32
    dma = pltpu.SemaphoreType.DMA
    return pl.pallas_call(
        functools.partial(kernel, n_cp, n_tp),
        out_shape=pltpu.VMEM((held, tokens, width), bf16),
        in_specs=[pl.BlockSpec(memory_space=pltpu.HBM)] * 6,
        out_specs=pl.BlockSpec(memory_space=pltpu.VMEM),
        scratch_shapes=[
            pltpu.VMEM((held, tokens, width), bf16),
            pltpu.VMEM((held, reach, kv_width), bf16),
            pltpu.VMEM((held, reach, kv_width), bf16),
            pltpu.VMEM(key_rows.shape, bf16),
            pltpu.VMEM(key_rows.shape, bf16),
            pltpu.VMEM(key_rows.shape, bf16),
            pltpu.VMEM(key_rows.shape, bf16),
            pltpu.VMEM((2, tokens, kv_width), bf16),
            pltpu.VMEM((tokens, width), bf16),
            pltpu.VMEM((held, tokens), i32),
            pltpu.VMEM((held, tokens, 128), i32),
            pltpu.SMEM(source_lists.shape, i32),
            pltpu.SMEM(slot_block.shape, i32),
            dma((3,)),
            dma((2,)),
            dma((3,)),
            dma((2, n_tp)),
            dma((2, n_tp)),
            dma((n_tp,)),
            dma((n_tp,)),
            dma((8 + 4 * len(ASIDE), 2)),
            dma((4, 2)),
            dma((2,)),
            dma((len(ASIDE), n_tp)),
            pltpu.SemaphoreType.REGULAR((2 + 4 * len(ASIDE),)),
        ],
        compiler_params=pltpu.CompilerParams(
            collective_id=0, has_side_effects=True, vmem_limit_bytes=40 * 1024 * 1024
        ),
        name="attention",
    )(*(pltpu.with_memory_space_constraint(operand, pltpu.HBM) for operand in operands))


def solution(mesh):
    in_specs = (
        P("cp", "tp", None),
        P("cp", "tp", None),
        P("cp", "tp", None),
        P("cp", None),
        P("cp", None),
        P(),
    )
    out_specs = P("cp", None, "tp")
    return jax.shard_map(
        functools.partial(on_device, mesh.shape["cp"], mesh.shape["tp"]),
        mesh=mesh,
        in_specs=in_specs,
        out_specs=out_specs,
        check_vma=False,
    )
```

```python
import functools

import jax
import jax.numpy as jnp
from jax import lax
from jax.experimental import pallas as pl
from jax.experimental.pallas import tpu as pltpu
from jax.sharding import PartitionSpec as P

QUERY_HEAD_COUNT = 64
KEY_VALUE_HEADS = 8
HEAD_SIZE = 128
LIST = 2
MESH = pl.DeviceIdType.MESH

neg_large = -1e30
SCALE = HEAD_SIZE ** (-0.5) * 1.4426950408889634
RUN = 2
ORDER = (1, 2, 6, 3, 7, 4, 5)
AHEAD = 3
SCHEDULE = (
    (("a", (0, 1)), ("a", (2, 3))),
    "keys",
    (("b", (0, 1)), ("b", (2, 3))),
    (("a", (6, 7)), ("b", (6, 7))),
    (("a", (4, 5)), ("b", (4, 5))),
)
GROUP = 16
ASIDE = ((15, 0, 1, 0), (15, 1, 1, 0), (14, 0, 16, -14), (14, 1, 14, -12))


def kernel(
    n_cp,
    n_tp,
    q_hbm,
    k_hbm,
    v_hbm,
    start_hbm,
    list_hbm,
    slot_hbm,
    out_ref,
    q_all,
    k_all,
    v_all,
    k_raw,
    v_raw,
    k_cut,
    v_cut,
    relay,
    done,
    start_buf,
    low_bound,
    list_buf,
    slot_buf,
    small_sem,
    raw_sem,
    own_sem,
    kv_send,
    kv_recv,
    q_send,
    q_recv,
    far_send,
    far_recv,
    relay_recv,
    cross_send,
    answer,
):
    held, part, _ = q_hbm.shape
    tokens = part * n_tp
    width = q_hbm.shape[2] // n_tp
    kv_width = k_hbm.shape[2] // n_tp
    group = width // HEAD_SIZE
    window = LIST * tokens + tokens // 2
    c = lax.axis_index("cp")
    t = lax.axis_index("tp")
    n_x = n_tp // RUN
    x, z = t // RUN, t % RUN

    def peer(offset, sign):
        dx, dz = offset // RUN, offset % RUN
        return ((x + sign * dx + n_x) % n_x) * RUN + (z + sign * dz + RUN) % RUN

    def climbs(who, place):
        return (who >= 0) & (who + GROUP < n_cp) & ((who + 2 * GROUP) % GROUP == place)

    def descends(who, place):
        return (who >= GROUP) & (who < n_cp) & (who % GROUP == GROUP - 1 - place)

    even = c % 2 == 0
    odd = c % 2 == 1

    pairs = []

    def pair(holds, distance, whole=False):
        if distance > 0:
            pairs.append((holds(c), holds(c - distance), distance, True, False))
        else:
            pairs.append((holds(c - distance), holds(c), -distance, False, whole))
        return len(pairs) - 1

    near = [pair(lambda who, d=d: (who >= 0) & (who + d < n_cp), d) for d in (1, 2)]
    outward, onward = {}, {}
    for place, which, leg, rest in ASIDE:
        for goes, way in ((climbs, 1), (descends, -1)):
            go = functools.partial(goes, place=place)
            outward[place, which, way] = pair(go, way * leg, True)
            if rest:
                onward[place, which, way] = pair(lambda who, go=go, leg=way * leg: go(who - leg), way * rest)

    barrier = pltpu.get_barrier_semaphore()
    for offset in range(1, n_tp):
        pl.semaphore_signal(
            barrier, inc=1, device_id=(c, peer(offset, 1)), device_id_type=MESH
        )
    greeted = n_tp - 1

    for is_lower, is_upper, distance, _, whole in pairs:
        greeted = greeted + jnp.where(is_upper, n_tp if whole else 1, 0)

        @pl.when(is_lower)
        def _():
            for to in range(n_tp) if whole else (t,):
                pl.semaphore_signal(
                    barrier, inc=1, device_id=(c + distance, to), device_id_type=MESH
                )

    def answered(number):
        @pl.when(pairs[number][0])
        def _():
            pl.semaphore_wait(answer.at[number], 1)

    small = [
        pltpu.make_async_copy(slot_hbm, slot_buf, small_sem.at[0]),
        pltpu.make_async_copy(start_hbm, start_buf, small_sem.at[1]),
        pltpu.make_async_copy(list_hbm, list_buf, small_sem.at[2]),
    ]
    raw = [
        pltpu.make_async_copy(k_hbm, k_raw, raw_sem.at[0]),
        pltpu.make_async_copy(v_hbm, v_raw, raw_sem.at[1]),
    ]
    own_rows = pl.ds(pl.multiple_of(t * part, part), part)
    own_key_rows = pl.ds(pl.multiple_of(LIST * tokens + t * part, part), part)

    def cut(ref, size, which):
        return ref.at[:, :, pl.ds(pl.multiple_of(which * size, size), size)]

    own = [
        pltpu.make_async_copy(cut(k_cut, kv_width, t), k_all.at[:, own_key_rows], own_sem.at[0]),
        pltpu.make_async_copy(cut(v_cut, kv_width, t), v_all.at[:, own_key_rows], own_sem.at[1]),
        pltpu.make_async_copy(cut(q_hbm, width, t), q_all.at[:, own_rows], own_sem.at[2]),
    ]
    for copy in small[:1] + raw + small[1:] + own[2:]:
        copy.start()

    small[0].wait()
    block_ids = [slot_buf[c * held + s] for s in range(held)]
    swapped = block_ids[0] >= n_cp

    def in_place(place, of_slot):
        return jnp.where(swapped, of_slot(1 - place), of_slot(place))

    for which, (ref, dst) in enumerate(((k_raw, k_cut), (v_raw, v_cut))):
        raw[which].wait()
        for place in range(held):
            dst[place] = in_place(place, lambda s: ref[s])
        own[which].start()
    pl.semaphore_wait(barrier, greeted)
    for number, (_, is_upper, distance, sends, _) in enumerate(pairs):

        @pl.when(is_upper & sends)
        def _():
            pl.semaphore_signal(
                answer.at[number], inc=1, device_id=(c - distance, t), device_id_type=MESH
            )

    kv_copies = ([], [])
    q_copies = {}
    for which, (ref, dst) in enumerate(((k_cut, k_all), (v_cut, v_all))):
        for offset in ORDER:
            to = peer(offset, 1)
            copy = pltpu.make_async_remote_copy(
                src_ref=cut(ref, kv_width, to),
                dst_ref=dst.at[:, own_key_rows],
                send_sem=kv_send.at[which, offset],
                recv_sem=kv_recv.at[which, offset],
                device_id=(c, to),
                device_id_type=MESH,
            )
            copy.start()
            kv_copies[which].append(copy)
    def segment(place, below):
        rows = pl.ds((LIST - below) * tokens, tokens)
        return [k_all.at[place, rows], v_all.at[place, rows]]

    low, high = segment(0, 0), segment(1, 0)
    low_1, low_2, high_1, high_2 = segment(0, 1), segment(0, 2), segment(1, 1), segment(1, 2)
    low_1_in, low_2_in, high_1_in, high_2_in = [
        [far_recv.at[i, which] for which in range(2)] for i in range(4)
    ]
    aside, aside_in = [relay.at[0], relay.at[1]], [relay_recv.at[0], relay_recv.at[1]]

    edge = GROUP - 1
    crossing = {1: [], -1: []}
    for number, (place, which, leg, rest) in enumerate(ASIDE):
        for goes, way, side in ((climbs, 1, 0), (descends, -1, 1)):
            dst, recv = aside[which], aside_in[which]
            if not rest:
                dst, recv = ((low_1, low_1_in), (high_1, high_1_in))[side]
                dst, recv = dst[which], recv[which]
            copies = [
                pltpu.make_async_remote_copy(
                    src_ref=(k_cut, v_cut)[which].at[side, :, pl.ds(to * kv_width, kv_width)],
                    dst_ref=dst.at[own_rows],
                    send_sem=cross_send.at[number, to],
                    recv_sem=recv,
                    device_id=(c + way * leg, to),
                    device_id_type=MESH,
                )
                for to in range(n_tp)
            ]
            crossing[way].append((goes(c, place), (place, which, way), copies))

    def cross(way):
        for when, key, copies in crossing[way]:
            if way > 0:
                answered(outward[key])

            @pl.when(when)
            def _():
                for copy in copies:
                    copy.start()

    cross(-1)
    for offset in ORDER:
        to = peer(offset, 1)
        q_copies[offset] = pltpu.make_async_remote_copy(
            src_ref=cut(q_hbm, width, to),
            dst_ref=q_all.at[:, own_rows],
            send_sem=q_send.at[offset],
            recv_sem=q_recv.at[offset],
            device_id=(c, to),
            device_id_type=MESH,
        )

    crosses_up = (c + GROUP < n_cp) & (c % GROUP >= edge - 1)
    for offset in ORDER[:AHEAD]:
        q_copies[offset].start()

    @pl.when(~crosses_up)
    def _():
        for offset in ORDER[AHEAD:]:
            q_copies[offset].start()

    cross(1)

    @pl.when(crosses_up)
    def _():
        for offset in ORDER[AHEAD:]:
            q_copies[offset].start()

    for copy in small[1:]:
        copy.wait()

    def lowest_of(s):
        named = jnp.int32(0)
        for entry in range(LIST):
            named = named + jnp.where(list_buf[s, entry] >= 0, tokens, 0)
        return jnp.maximum(start_buf[s : s + 1, :] - block_ids[s] * tokens, -named)

    for place in range(held):
        row = in_place(place, lowest_of)
        for at in range(0, tokens, 128):
            low_bound[place, at : at + 128, :] = jnp.broadcast_to(
                row[:, at : at + 128], (128, 128)
            ).T

    def far(which, src, dst, order, recv, distance):
        return pltpu.make_async_remote_copy(
            src_ref=src[which],
            dst_ref=dst[which],
            send_sem=far_send.at[order, which],
            recv_sem=recv[which],
            device_id=(c + distance, t),
            device_id_type=MESH,
        )

    last = c == n_cp - 1
    hand_low, hand_high = even & (c >= 2), odd
    both = (0, 1)
    first = [
        (both, (c + 1 < n_cp) & ~climbs(c, edge), low, low_1, low_1_in, 1),
        (both, (c >= 1) & ~descends(c, edge), high, high_1, high_1_in, -1),
        (both, even & (c + 2 < n_cp) & ~climbs(c, edge - 1), low, low_2, low_2_in, 2),
        (both, odd & (c >= 2) & ~descends(c, edge - 1), high, high_2, high_2_in, -2),
    ]
    passed = []
    for place, which, leg, rest in ASIDE:
        if rest:
            to_low, to_high = (low_1, high_1) if place == edge else (low_2, high_2)
            in_low, in_high = (low_1_in, high_1_in) if place == edge else (low_2_in, high_2_in)
            passed += [
                ((which,), climbs(c - leg, place), aside, to_low, in_low, rest),
                ((which,), descends(c + leg, place), aside, to_high, in_high, -rest),
            ]
    handed = [
        (both, hand_low, low_1, low_2, low_2_in, 1),
        (both, hand_high, high_1, high_2, high_2_in, -1),
    ]
    moves = [(order,) + move for order, move in enumerate(first + passed + handed)]
    ways = [(place, which, way) for place, which, _, rest in ASIDE if rest for way in (1, -1)]
    waits = {len(first) + i: onward[key] for i, key in enumerate(ways)}
    first, passed, handed = moves[: len(first)], moves[len(first) : -2], moves[-2:]

    def send(move, which):
        order, whiches, when, src, dst, recv, distance = move
        if which in whiches:
            if order in waits and distance > 0:
                answered(waits[order])

            @pl.when(when)
            def _():
                far(which, src, dst, order, recv, distance).start()

    def arrive(when, which, dst, recv):
        @pl.when(when)
        def _():
            far(which, dst, dst, 0, recv, 0).wait_recv()

    def hand_on(which):
        arrive(hand_low, which, low_1, low_1_in)
        arrive(hand_high & ~last, which, high_1, high_1_in)
        for move in handed:
            send(move, which)

    for which in range(2):
        own[which].wait()
        for copy in kv_copies[which]:
            copy.wait_recv()
        for move in first:
            if move[-1] < 0:
                send(move, which)
        if which == 0:
            for number in near:
                answered(number)
        for move in first:
            if move[-1] > 0:
                send(move, which)
    for which in range(2):

        @pl.when(c < 1)
        def _():
            low_1[which][...] = jnp.zeros((tokens, kv_width), k_all.dtype)

        @pl.when(c < 2)
        def _():
            low_2[which][...] = jnp.zeros((tokens, kv_width), k_all.dtype)

        @pl.when(last)
        def _():
            high_1[which][...] = low[which][...]

    for which in range(2):
        for move in passed:
            if which in move[1]:
                arrive(move[2], which, aside, aside_in)
            send(move, which)
    for which in range(2):
        hand_on(which)

    place_a = jnp.where(c % GROUP < 2, 1, 0)
    place_b = 1 - place_a

    def keys_in(place):
        for which in range(2):
            arrive((place == 0) & odd, which, low_1, low_1_in)
            arrive((place == 0) & (c >= 2), which, low_2, low_2_in)
            arrive((place == 1) & even, which, high_1, high_1_in)
            arrive((place == 1) & ~last, which, high_2, high_2_in)

            @pl.when((place == 1) & last)
            def _():
                high_2[which][...] = low_1[which][...]

    def attend(place, start, size, half):
        rows = pl.ds(pl.multiple_of(start, size), size)
        slot = jnp.where(swapped, 1 - place, place)
        begin = half * (tokens // 2)
        keys = pl.ds(pl.multiple_of(begin, tokens // 2), window)
        lane = lax.broadcasted_iota(jnp.int32, (size, 128), 1)
        sub = lax.broadcasted_iota(jnp.int32, (size, 128), 0)
        query = jnp.where(slot == 0, q_all[0, rows, :], q_all[1, rows, :])
        query = jnp.concatenate(
            [query[:, h * HEAD_SIZE : (h + 1) * HEAD_SIZE] for h in range(group)], axis=0
        )
        scores = lax.dot_general(
            query, k_all[place, keys, :], (((1,), (1,)), ((), ())), preferred_element_type=jnp.float32
        )
        lowest = low_bound[place, rows, :]
        highest = sub + start
        visible = []
        for at in range(0, window, 128):
            key = lane + (begin + at - LIST * tokens)
            visible.append((key >= lowest) & (key <= highest))
        visible = jnp.concatenate(visible, axis=1)
        scores = scores.reshape(group, size, window)
        scores = jnp.where(visible[None], scores, neg_large)
        scores = scores.reshape(group * size, window)
        best = jnp.max(scores, axis=-1, keepdims=True)
        weights = jnp.exp2((scores - best) * SCALE)
        total = jnp.sum(weights, axis=-1, keepdims=True)
        mixed = jnp.dot(
            weights.astype(jnp.bfloat16), v_all[place, keys, :], preferred_element_type=jnp.float32
        )
        mixed = (mixed * (1.0 / total)).astype(jnp.bfloat16)
        return jnp.concatenate([mixed[h * size : (h + 1) * size] for h in range(group)], axis=1)

    def part_of(offsets):
        source_x = (x - offsets[0] // RUN + n_x) % n_x
        source = source_x * RUN if len(offsets) == RUN else peer(offsets[0], -1)
        return source * part, len(offsets) * part, source_x // (n_x // 2)

    own[2].wait()
    keys_in(place_a)
    arrived = {0}
    def all_but_queries_sent():
        for copy in kv_copies[0] + kv_copies[1]:
            copy.wait_send()
        for when, _, copies in crossing[1] + crossing[-1]:

            @pl.when(when)
            def _():
                for copy in copies:
                    copy.wait_send()

        for order, whiches, when, src, dst, recv, distance in moves:

            @pl.when(when)
            def _():
                for which in whiches:
                    far(which, src, dst, order, recv, distance).wait_send()

    for step in SCHEDULE:
        if step is SCHEDULE[-1]:
            all_but_queries_sent()
        if step == "keys":
            keys_in(place_b)
            continue
        for _, offsets in step:
            for offset in offsets:
                if offset not in arrived:
                    arrived.add(offset)
                    q_copies[offset].wait_recv()
        results = {}
        for turn, offsets in step:
            place = place_a if turn == "a" else place_b
            start, size, half = part_of(offsets)
            results[turn, offsets] = start, size, attend(place, start, size, half)
        for (turn, offsets), (start, size, result) in results.items():
            rows = pl.ds(pl.multiple_of(start, size), size)
            if turn == "b":
                result_a = results["a", offsets][2] if ("a", offsets) in results else done[rows, :]
                b_is_0 = swapped == (place_b == 1)
                out_ref[0, rows, :] = jnp.where(b_is_0, result, result_a)
                out_ref[1, rows, :] = jnp.where(b_is_0, result_a, result)
            elif ("b", offsets) not in results:
                done[rows, :] = result

    for copy in q_copies.values():
        copy.wait_send()


def on_device(n_cp, n_tp, *operands):
    query_rows, key_rows, _, _, source_lists, slot_block = operands
    held, part, all_width = query_rows.shape
    tokens = part * n_tp
    width = all_width // n_tp
    kv_width = key_rows.shape[2] // n_tp
    reach = (LIST + 1) * tokens
    bf16, i32 = jnp.bfloat16, jnp.int32
    dma = pltpu.SemaphoreType.DMA
    return pl.pallas_call(
        functools.partial(kernel, n_cp, n_tp),
        out_shape=pltpu.VMEM((held, tokens, width), bf16),
        in_specs=[pl.BlockSpec(memory_space=pltpu.HBM)] * 6,
        out_specs=pl.BlockSpec(memory_space=pltpu.VMEM),
        scratch_shapes=[
            pltpu.VMEM((held, tokens, width), bf16),
            pltpu.VMEM((held, reach, kv_width), bf16),
            pltpu.VMEM((held, reach, kv_width), bf16),
            pltpu.VMEM(key_rows.shape, bf16),
            pltpu.VMEM(key_rows.shape, bf16),
            pltpu.VMEM(key_rows.shape, bf16),
            pltpu.VMEM(key_rows.shape, bf16),
            pltpu.VMEM((2, tokens, kv_width), bf16),
            pltpu.VMEM((tokens, width), bf16),
            pltpu.VMEM((held, tokens), i32),
            pltpu.VMEM((held, tokens, 128), i32),
            pltpu.SMEM(source_lists.shape, i32),
            pltpu.SMEM(slot_block.shape, i32),
            dma((3,)),
            dma((2,)),
            dma((3,)),
            dma((2, n_tp)),
            dma((2, n_tp)),
            dma((n_tp,)),
            dma((n_tp,)),
            dma((8 + 4 * len(ASIDE), 2)),
            dma((4, 2)),
            dma((2,)),
            dma((len(ASIDE), n_tp)),
            pltpu.SemaphoreType.REGULAR((2 + 4 * len(ASIDE),)),
        ],
        compiler_params=pltpu.CompilerParams(
            collective_id=0, has_side_effects=True, vmem_limit_bytes=40 * 1024 * 1024
        ),
        name="attention",
    )(*(pltpu.with_memory_space_constraint(operand, pltpu.HBM) for operand in operands))


def solution(mesh):
    in_specs = (
        P("cp", "tp", None),
        P("cp", "tp", None),
        P("cp", "tp", None),
        P("cp", None),
        P("cp", None),
        P(),
    )
    out_specs = P("cp", None, "tp")
    return jax.shard_map(
        functools.partial(on_device, mesh.shape["cp"], mesh.shape["tp"]),
        mesh=mesh,
        in_specs=in_specs,
        out_specs=out_specs,
        check_vma=False,
    )
```

```python
import functools

import jax
import jax.numpy as jnp
from jax import lax
from jax.experimental import pallas as pl
from jax.experimental.pallas import tpu as pltpu
from jax.sharding import PartitionSpec as P

QUERY_HEAD_COUNT = 64
KEY_VALUE_HEADS = 8
HEAD_SIZE = 128
LIST = 2
MESH = pl.DeviceIdType.MESH

neg_large = -1e30
SCALE = HEAD_SIZE ** (-0.5) * 1.4426950408889634
RUN = 2
ORDER = (1, 2, 6, 3, 7, 4, 5)
AHEAD = 3
SCHEDULE = (
    (("a", (0, 1)), ("a", (2, 3))),
    "keys",
    (("b", (0, 1)), ("b", (2, 3))),
    (("a", (6, 7)), ("b", (6, 7))),
    (("a", (4, 5)), ("b", (4, 5))),
)
GROUP = 16
ASIDE = ((14, 0, 16, -14), (14, 1, 14, -12), (15, 0, 1, 0), (15, 1, 3, -2))


def kernel(
    n_cp,
    n_tp,
    q_hbm,
    k_hbm,
    v_hbm,
    start_hbm,
    list_hbm,
    slot_hbm,
    out_ref,
    q_all,
    k_all,
    v_all,
    k_raw,
    v_raw,
    k_cut,
    v_cut,
    relay,
    done,
    start_buf,
    low_bound,
    list_buf,
    slot_buf,
    small_sem,
    raw_sem,
    own_sem,
    kv_send,
    kv_recv,
    q_send,
    q_recv,
    far_send,
    far_recv,
    relay_recv,
    cross_send,
    answer,
):
    held, part, _ = q_hbm.shape
    tokens = part * n_tp
    width = q_hbm.shape[2] // n_tp
    kv_width = k_hbm.shape[2] // n_tp
    group = width // HEAD_SIZE
    window = LIST * tokens + tokens // 2
    c = lax.axis_index("cp")
    t = lax.axis_index("tp")
    n_x = n_tp // RUN
    x, z = t // RUN, t % RUN

    def peer(offset, sign):
        dx, dz = offset // RUN, offset % RUN
        return ((x + sign * dx + n_x) % n_x) * RUN + (z + sign * dz + RUN) % RUN

    def climbs(who, place):
        return (who >= 0) & (who + GROUP < n_cp) & ((who + 2 * GROUP) % GROUP == place)

    def descends(who, place):
        return (who >= GROUP) & (who < n_cp) & (who % GROUP == GROUP - 1 - place)

    even = c % 2 == 0
    odd = c % 2 == 1

    pairs = []

    def pair(holds, distance, whole=False):
        if distance > 0:
            pairs.append((holds(c), holds(c - distance), distance, True, False))
        else:
            pairs.append((holds(c - distance), holds(c), -distance, False, whole))
        return len(pairs) - 1

    near = [pair(lambda who, d=d: (who >= 0) & (who + d < n_cp), d) for d in (1, 2)]
    outward, onward = {}, {}
    for place, which, leg, rest in ASIDE:
        for goes, way in ((climbs, 1), (descends, -1)):
            go = functools.partial(goes, place=place)
            outward[place, which, way] = pair(go, way * leg, True)
            if rest:
                onward[place, which, way] = pair(lambda who, go=go, leg=way * leg: go(who - leg), way * rest)

    barrier = pltpu.get_barrier_semaphore()
    for offset in range(1, n_tp):
        pl.semaphore_signal(
            barrier, inc=1, device_id=(c, peer(offset, 1)), device_id_type=MESH
        )
    greeted = n_tp - 1

    for is_lower, is_upper, distance, _, whole in pairs:
        greeted = greeted + jnp.where(is_upper, n_tp if whole else 1, 0)

        @pl.when(is_lower)
        def _():
            for to in range(n_tp) if whole else (t,):
                pl.semaphore_signal(
                    barrier, inc=1, device_id=(c + distance, to), device_id_type=MESH
                )

    def answered(number):
        @pl.when(pairs[number][0])
        def _():
            pl.semaphore_wait(answer.at[number], 1)

    small = [
        pltpu.make_async_copy(slot_hbm, slot_buf, small_sem.at[0]),
        pltpu.make_async_copy(start_hbm, start_buf, small_sem.at[1]),
        pltpu.make_async_copy(list_hbm, list_buf, small_sem.at[2]),
    ]
    raw = [
        pltpu.make_async_copy(k_hbm, k_raw, raw_sem.at[0]),
        pltpu.make_async_copy(v_hbm, v_raw, raw_sem.at[1]),
    ]
    own_rows = pl.ds(pl.multiple_of(t * part, part), part)
    own_key_rows = pl.ds(pl.multiple_of(LIST * tokens + t * part, part), part)

    def cut(ref, size, which):
        return ref.at[:, :, pl.ds(pl.multiple_of(which * size, size), size)]

    own = [
        pltpu.make_async_copy(cut(k_cut, kv_width, t), k_all.at[:, own_key_rows], own_sem.at[0]),
        pltpu.make_async_copy(cut(v_cut, kv_width, t), v_all.at[:, own_key_rows], own_sem.at[1]),
        pltpu.make_async_copy(cut(q_hbm, width, t), q_all.at[:, own_rows], own_sem.at[2]),
    ]
    for copy in small[:1] + raw + small[1:] + own[2:]:
        copy.start()

    small[0].wait()
    block_ids = [slot_buf[c * held + s] for s in range(held)]
    swapped = block_ids[0] >= n_cp

    def in_place(place, of_slot):
        return jnp.where(swapped, of_slot(1 - place), of_slot(place))

    for which, (ref, dst) in enumerate(((k_raw, k_cut), (v_raw, v_cut))):
        raw[which].wait()
        for place in range(held):
            dst[place] = in_place(place, lambda s: ref[s])
        own[which].start()
    pl.semaphore_wait(barrier, greeted)
    for number, (_, is_upper, distance, sends, _) in enumerate(pairs):

        @pl.when(is_upper & sends)
        def _():
            pl.semaphore_signal(
                answer.at[number], inc=1, device_id=(c - distance, t), device_id_type=MESH
            )

    kv_copies = ([], [])
    q_copies = {}
    for which, (ref, dst) in enumerate(((k_cut, k_all), (v_cut, v_all))):
        for offset in ORDER:
            to = peer(offset, 1)
            copy = pltpu.make_async_remote_copy(
                src_ref=cut(ref, kv_width, to),
                dst_ref=dst.at[:, own_key_rows],
                send_sem=kv_send.at[which, offset],
                recv_sem=kv_recv.at[which, offset],
                device_id=(c, to),
                device_id_type=MESH,
            )
            copy.start()
            kv_copies[which].append(copy)
    def segment(place, below):
        rows = pl.ds((LIST - below) * tokens, tokens)
        return [k_all.at[place, rows], v_all.at[place, rows]]

    low, high = segment(0, 0), segment(1, 0)
    low_1, low_2, high_1, high_2 = segment(0, 1), segment(0, 2), segment(1, 1), segment(1, 2)
    low_1_in, low_2_in, high_1_in, high_2_in = [
        [far_recv.at[i, which] for which in range(2)] for i in range(4)
    ]
    aside, aside_in = [relay.at[0], relay.at[1]], [relay_recv.at[0], relay_recv.at[1]]

    edge = GROUP - 1
    crossing = {1: [], -1: []}
    for number, (place, which, leg, rest) in enumerate(ASIDE):
        for goes, way, side in ((climbs, 1, 0), (descends, -1, 1)):
            dst, recv = aside[which], aside_in[which]
            if not rest:
                dst, recv = ((low_1, low_1_in), (high_1, high_1_in))[side]
                dst, recv = dst[which], recv[which]
            copies = [
                pltpu.make_async_remote_copy(
                    src_ref=(k_cut, v_cut)[which].at[side, :, pl.ds(to * kv_width, kv_width)],
                    dst_ref=dst.at[own_rows],
                    send_sem=cross_send.at[number, to],
                    recv_sem=recv,
                    device_id=(c + way * leg, to),
                    device_id_type=MESH,
                )
                for to in range(n_tp)
            ]
            crossing[way].append((goes(c, place), (place, which, way), copies))

    def cross(way):
        for when, key, copies in crossing[way]:
            if way > 0:
                answered(outward[key])

            @pl.when(when)
            def _():
                for copy in copies:
                    copy.start()

    cross(-1)
    for offset in ORDER:
        to = peer(offset, 1)
        q_copies[offset] = pltpu.make_async_remote_copy(
            src_ref=cut(q_hbm, width, to),
            dst_ref=q_all.at[:, own_rows],
            send_sem=q_send.at[offset],
            recv_sem=q_recv.at[offset],
            device_id=(c, to),
            device_id_type=MESH,
        )

    crosses_up = (c + GROUP < n_cp) & (c % GROUP >= edge - 1)
    for offset in ORDER[:AHEAD]:
        q_copies[offset].start()

    @pl.when(~crosses_up)
    def _():
        for offset in ORDER[AHEAD:]:
            q_copies[offset].start()

    cross(1)

    @pl.when(crosses_up)
    def _():
        for offset in ORDER[AHEAD:]:
            q_copies[offset].start()

    for copy in small[1:]:
        copy.wait()

    def lowest_of(s):
        named = jnp.int32(0)
        for entry in range(LIST):
            named = named + jnp.where(list_buf[s, entry] >= 0, tokens, 0)
        return jnp.maximum(start_buf[s : s + 1, :] - block_ids[s] * tokens, -named)

    for place in range(held):
        row = in_place(place, lowest_of)
        for at in range(0, tokens, 128):
            low_bound[place, at : at + 128, :] = jnp.broadcast_to(
                row[:, at : at + 128], (128, 128)
            ).T

    def far(which, src, dst, order, recv, distance):
        return pltpu.make_async_remote_copy(
            src_ref=src[which],
            dst_ref=dst[which],
            send_sem=far_send.at[order, which],
            recv_sem=recv[which],
            device_id=(c + distance, t),
            device_id_type=MESH,
        )

    last = c == n_cp - 1
    hand_low, hand_high = even & (c >= 2), odd
    both = (0, 1)
    first = [
        (both, (c + 1 < n_cp) & ~climbs(c, edge), low, low_1, low_1_in, 1),
        (both, (c >= 1) & ~descends(c, edge), high, high_1, high_1_in, -1),
        (both, even & (c + 2 < n_cp) & ~climbs(c, edge - 1), low, low_2, low_2_in, 2),
        (both, odd & (c >= 2) & ~descends(c, edge - 1), high, high_2, high_2_in, -2),
    ]
    passed = []
    for place, which, leg, rest in ASIDE:
        if rest:
            to_low, to_high = (low_1, high_1) if place == edge else (low_2, high_2)
            in_low, in_high = (low_1_in, high_1_in) if place == edge else (low_2_in, high_2_in)
            passed += [
                ((which,), climbs(c - leg, place), aside, to_low, in_low, rest),
                ((which,), descends(c + leg, place), aside, to_high, in_high, -rest),
            ]
    handed = [
        (both, hand_low, low_1, low_2, low_2_in, 1),
        (both, hand_high, high_1, high_2, high_2_in, -1),
    ]
    moves = [(order,) + move for order, move in enumerate(first + passed + handed)]
    ways = [(place, which, way) for place, which, _, rest in ASIDE if rest for way in (1, -1)]
    waits = {len(first) + i: onward[key] for i, key in enumerate(ways)}
    first, passed, handed = moves[: len(first)], moves[len(first) : -2], moves[-2:]

    def send(move, which):
        order, whiches, when, src, dst, recv, distance = move
        if which in whiches:
            if order in waits and distance > 0:
                answered(waits[order])

            @pl.when(when)
            def _():
                far(which, src, dst, order, recv, distance).start()

    def arrive(when, which, dst, recv):
        @pl.when(when)
        def _():
            far(which, dst, dst, 0, recv, 0).wait_recv()

    def hand_on(which):
        arrive(hand_low, which, low_1, low_1_in)
        arrive(hand_high & ~last, which, high_1, high_1_in)
        for move in handed:
            send(move, which)

    for which in range(2):
        own[which].wait()
        for copy in kv_copies[which]:
            copy.wait_recv()
        for move in first:
            if move[-1] < 0:
                send(move, which)
        if which == 0:
            for number in near:
                answered(number)
        for move in first:
            if move[-1] > 0:
                send(move, which)
    for which in range(2):

        @pl.when(c < 1)
        def _():
            low_1[which][...] = jnp.zeros((tokens, kv_width), k_all.dtype)

        @pl.when(c < 2)
        def _():
            low_2[which][...] = jnp.zeros((tokens, kv_width), k_all.dtype)

        @pl.when(last)
        def _():
            high_1[which][...] = low[which][...]

    for which in range(2):
        for move in passed:
            if which in move[1]:
                arrive(move[2], which, aside, aside_in)
            send(move, which)
    for which in range(2):
        hand_on(which)

    place_a = jnp.where(c % GROUP < 2, 1, 0)
    place_b = 1 - place_a

    def keys_in(place):
        for which in range(2):
            arrive((place == 0) & odd, which, low_1, low_1_in)
            arrive((place == 0) & (c >= 2), which, low_2, low_2_in)
            arrive((place == 1) & even, which, high_1, high_1_in)
            arrive((place == 1) & ~last, which, high_2, high_2_in)

            @pl.when((place == 1) & last)
            def _():
                high_2[which][...] = low_1[which][...]

    def attend(place, start, size, half):
        rows = pl.ds(pl.multiple_of(start, size), size)
        slot = jnp.where(swapped, 1 - place, place)
        begin = half * (tokens // 2)
        keys = pl.ds(pl.multiple_of(begin, tokens // 2), window)
        lane = lax.broadcasted_iota(jnp.int32, (size, 128), 1)
        sub = lax.broadcasted_iota(jnp.int32, (size, 128), 0)
        query = jnp.where(slot == 0, q_all[0, rows, :], q_all[1, rows, :])
        query = jnp.concatenate(
            [query[:, h * HEAD_SIZE : (h + 1) * HEAD_SIZE] for h in range(group)], axis=0
        )
        scores = lax.dot_general(
            query, k_all[place, keys, :], (((1,), (1,)), ((), ())), preferred_element_type=jnp.float32
        )
        lowest = low_bound[place, rows, :]
        highest = sub + start
        visible = []
        for at in range(0, window, 128):
            key = lane + (begin + at - LIST * tokens)
            visible.append((key >= lowest) & (key <= highest))
        visible = jnp.concatenate(visible, axis=1)
        scores = scores.reshape(group, size, window)
        scores = jnp.where(visible[None], scores, neg_large)
        scores = scores.reshape(group * size, window)
        best = jnp.max(scores, axis=-1, keepdims=True)
        weights = jnp.exp2((scores - best) * SCALE)
        total = jnp.sum(weights, axis=-1, keepdims=True)
        mixed = jnp.dot(
            weights.astype(jnp.bfloat16), v_all[place, keys, :], preferred_element_type=jnp.float32
        )
        mixed = (mixed * (1.0 / total)).astype(jnp.bfloat16)
        return jnp.concatenate([mixed[h * size : (h + 1) * size] for h in range(group)], axis=1)

    def part_of(offsets):
        source_x = (x - offsets[0] // RUN + n_x) % n_x
        source = source_x * RUN if len(offsets) == RUN else peer(offsets[0], -1)
        return source * part, len(offsets) * part, source_x // (n_x // 2)

    own[2].wait()
    keys_in(place_a)
    arrived = {0}
    def all_but_queries_sent():
        for copy in kv_copies[0] + kv_copies[1]:
            copy.wait_send()
        for when, _, copies in crossing[1] + crossing[-1]:

            @pl.when(when)
            def _():
                for copy in copies:
                    copy.wait_send()

        for order, whiches, when, src, dst, recv, distance in moves:

            @pl.when(when)
            def _():
                for which in whiches:
                    far(which, src, dst, order, recv, distance).wait_send()

    for step in SCHEDULE:
        if step is SCHEDULE[-1]:
            all_but_queries_sent()
        if step == "keys":
            keys_in(place_b)
            continue
        for _, offsets in step:
            for offset in offsets:
                if offset not in arrived:
                    arrived.add(offset)
                    q_copies[offset].wait_recv()
        results = {}
        for turn, offsets in step:
            place = place_a if turn == "a" else place_b
            start, size, half = part_of(offsets)
            results[turn, offsets] = start, size, attend(place, start, size, half)
        for (turn, offsets), (start, size, result) in results.items():
            rows = pl.ds(pl.multiple_of(start, size), size)
            if turn == "b":
                result_a = results["a", offsets][2] if ("a", offsets) in results else done[rows, :]
                b_is_0 = swapped == (place_b == 1)
                out_ref[0, rows, :] = jnp.where(b_is_0, result, result_a)
                out_ref[1, rows, :] = jnp.where(b_is_0, result_a, result)
            elif ("b", offsets) not in results:
                done[rows, :] = result

    for copy in q_copies.values():
        copy.wait_send()


def on_device(n_cp, n_tp, *operands):
    query_rows, key_rows, _, _, source_lists, slot_block = operands
    held, part, all_width = query_rows.shape
    tokens = part * n_tp
    width = all_width // n_tp
    kv_width = key_rows.shape[2] // n_tp
    reach = (LIST + 1) * tokens
    bf16, i32 = jnp.bfloat16, jnp.int32
    dma = pltpu.SemaphoreType.DMA
    return pl.pallas_call(
        functools.partial(kernel, n_cp, n_tp),
        out_shape=pltpu.VMEM((held, tokens, width), bf16),
        in_specs=[pl.BlockSpec(memory_space=pltpu.HBM)] * 6,
        out_specs=pl.BlockSpec(memory_space=pltpu.VMEM),
        scratch_shapes=[
            pltpu.VMEM((held, tokens, width), bf16),
            pltpu.VMEM((held, reach, kv_width), bf16),
            pltpu.VMEM((held, reach, kv_width), bf16),
            pltpu.VMEM(key_rows.shape, bf16),
            pltpu.VMEM(key_rows.shape, bf16),
            pltpu.VMEM(key_rows.shape, bf16),
            pltpu.VMEM(key_rows.shape, bf16),
            pltpu.VMEM((2, tokens, kv_width), bf16),
            pltpu.VMEM((tokens, width), bf16),
            pltpu.VMEM((held, tokens), i32),
            pltpu.VMEM((held, tokens, 128), i32),
            pltpu.SMEM(source_lists.shape, i32),
            pltpu.SMEM(slot_block.shape, i32),
            dma((3,)),
            dma((2,)),
            dma((3,)),
            dma((2, n_tp)),
            dma((2, n_tp)),
            dma((n_tp,)),
            dma((n_tp,)),
            dma((8 + 4 * len(ASIDE), 2)),
            dma((4, 2)),
            dma((2,)),
            dma((len(ASIDE), n_tp)),
            pltpu.SemaphoreType.REGULAR((2 + 4 * len(ASIDE),)),
        ],
        compiler_params=pltpu.CompilerParams(
            collective_id=0, has_side_effects=True, vmem_limit_bytes=40 * 1024 * 1024
        ),
        name="attention",
    )(*(pltpu.with_memory_space_constraint(operand, pltpu.HBM) for operand in operands))


def solution(mesh):
    in_specs = (
        P("cp", "tp", None),
        P("cp", "tp", None),
        P("cp", "tp", None),
        P("cp", None),
        P("cp", None),
        P(),
    )
    out_specs = P("cp", None, "tp")
    return jax.shard_map(
        functools.partial(on_device, mesh.shape["cp"], mesh.shape["tp"]),
        mesh=mesh,
        in_specs=in_specs,
        out_specs=out_specs,
        check_vma=False,
    )
```
